256 devices in a mesh: ctx: 32 (over z, y_hi, core), tp: 8 (over x, y_lo).
Axes of the slice: x: 4, y: 4 (y_hi: 2, y_lo: 2; y = y_hi * 2 + y_lo), z: 8, core: 2. Of those that a mesh axis runs over, the one named last changes fastest.
Arguments:
- queries: bfloat16 [4096, 8192], P('ctx', 'tp'), may hold values from -4.375 to 4.375
- stored_keys: bfloat16 [8192, 1024], P('ctx', 'tp'), may hold values from -4.375 to 4.375
- stored_values: bfloat16 [8192, 1024], P('ctx', 'tp'), may hold values from -6 to 6
- fresh_keys: bfloat16 [4096, 1024], P('ctx', 'tp'), may hold values from -6 to 6
- fresh_values: bfloat16 [4096, 1024], P('ctx', 'tp'), may hold values from -6 to 6
- cache_lengths: int32 [32], replicated, may hold values from 1 to 256, 5120 in all
- out_weight: bfloat16 [8192, 8192], P('tp', 'ctx'), may hold values from -0.0625 to 0.0625
Outputs:
- mixed: bfloat16 [4096, 8192], P('tp', 'ctx')
The draws below stay inside these ranges and needn't reach their ends.
Inputs may be any that keep to these rules, and one draw needn't show every extreme that they name: `cache_lengths`: the longest shard holds exactly 256 used positions.
All inputs are finite; a program needn't handle non-finite values.
Results may differ from the reference program's by a relative error of at most 0.02.
Values may be sent and summed in bfloat16 or wider, within the bound.
No kernel may reach another device: no remote copies, remote signals or barrier semaphores. Data moves between devices by JAX's collectives and lax.ppermute only.
A program may use at most 192 MiB of HBM per device.

```python
import math
import jax
import jax.numpy as jnp
import numpy as np
from jax import lax

D = 8192
QUERY_HEADS = 64
KEY_VALUE_HEADS = 8
HEAD_SIZE = 128
CACHE_DEV = 256
NEW_TOKEN_COUNT = 4096
CACHED_POSITIONS = 8192
N_CTX = 32


def draw_queries(key, part):
    key = jax.random.fold_in(key, 1)
    attention_output = jax.random.truncated_normal(jax.random.fold_in(key, 3), -4.0, 4.0, (NEW_TOKEN_COUNT, QUERY_HEADS * HEAD_SIZE), jnp.float32)
    return attention_output.astype(jnp.bfloat16)


def draw_stored_keys(key, part):
    key = jax.random.fold_in(key, 11)
    attention_output = jax.random.truncated_normal(jax.random.fold_in(key, 3), -4.0, 4.0, (CACHED_POSITIONS, KEY_VALUE_HEADS * HEAD_SIZE), jnp.float32)
    return attention_output.astype(jnp.bfloat16)


def level_of(key, shape, shards, least, largest):
    gain, own = 1.0, jax.random.fold_in(key, 6)
    for axis_at, parts in shards:
        steps = jnp.exp(jax.random.uniform(jax.random.fold_in(own, axis_at), (parts,), jnp.float32, least / len(shards), largest / len(shards)))
        gain = gain * jnp.repeat(steps, shape[axis_at] // parts).reshape([-1 if axis == axis_at else 1 for axis in range(len(shape))])
    return gain


def length_profile(count, total, bound, slope):
    portions = [(1 << 20) // math.isqrt(standing ** slope) + 1 for standing in range(2, count + 1)]
    rest, given = total - bound - (count - 1), [1] * (count - 1)
    while rest > 0:
        free = [i for i in range(count - 1) if given[i] < bound]
        whole, budget = sum([portions[i] for i in free]), rest
        for i in free:
            more = min(bound - given[i], max(1, budget * portions[i] // whole), rest)
            given[i] = given[i] + more
            rest = rest - more
    return np.array([bound] + given)


def ragged(rng, amount, total, reach, lean):
    if amount == 2:
        one = jax.random.randint(rng, (), max(1, total - reach), min(reach, total - 1) + 1)
        return jnp.stack([one, total - one])
    tallies = jnp.asarray(length_profile(amount, total, reach, lean), jnp.int32)
    pairs = (amount - 1) // 2
    giver, taker = tallies[1:1 + 2 * pairs:2], tallies[2:2 + 2 * pairs:2]
    room = jnp.minimum(giver - 1, reach - taker)
    shifted = jax.random.randint(jax.random.fold_in(rng, 1), (pairs,), 0, 1 << 20) % (room + 1)
    tallies = tallies.at[1:1 + 2 * pairs:2].set(giver - shifted).at[2:2 + 2 * pairs:2].set(taker + shifted)
    return tallies[jax.random.permutation(jax.random.fold_in(rng, 2), amount)]


def bell_draw(key, shape, spread, bound, cuts=(), kind=jnp.bfloat16):
    entries = spread * jax.random.normal(key, shape, jnp.float32)
    if cuts:
        entries = entries * level_of(key, shape, cuts, -0.22, 0.18)
    return jnp.clip(entries, -bound, bound).astype(kind)


def setup_inputs(seed: int = 0) -> dict:
    seeds = jax.random.split(jax.random.key(seed), 8)
    queries = draw_queries(jax.random.fold_in(seeds[7], 71), 0)
    stored_keys = draw_stored_keys(jax.random.fold_in(seeds[7], 71), 0)
    stored_values = bell_draw(seeds[2], (CACHED_POSITIONS, KEY_VALUE_HEADS * HEAD_SIZE), 1.0, 6.0, ((0, 32), (1, 8)))
    fresh_keys = bell_draw(seeds[3], (NEW_TOKEN_COUNT, KEY_VALUE_HEADS * HEAD_SIZE), 1.0, 6.0, ((0, 32), (1, 8)))
    fresh_values = bell_draw(seeds[4], (NEW_TOKEN_COUNT, KEY_VALUE_HEADS * HEAD_SIZE), 1.0, 6.0, ((0, 32), (1, 8)))
    cache_lengths = ragged(seeds[5], N_CTX, CACHE_DEV * N_CTX * 5 // 8, CACHE_DEV, 2).astype(jnp.int32)
    out_weight = bell_draw(seeds[6], (QUERY_HEADS * HEAD_SIZE, D), (QUERY_HEADS * HEAD_SIZE) ** -0.5, 0.0625, ((0, 8), (1, 32)))
    return dict(queries=queries, stored_keys=stored_keys, stored_values=stored_values, fresh_keys=fresh_keys, fresh_values=fresh_values, cache_lengths=cache_lengths, out_weight=out_weight)


def reference(queries, stored_keys, stored_values, fresh_keys, fresh_values, cache_lengths, out_weight):
    group_count = QUERY_HEADS // KEY_VALUE_HEADS
    score_scale = 1.0 / math.sqrt(HEAD_SIZE)
    total_key_length = CACHED_POSITIONS + NEW_TOKEN_COUNT
    merged_keys = jnp.concatenate([stored_keys, fresh_keys], 0).reshape(total_key_length, KEY_VALUE_HEADS, HEAD_SIZE).transpose(1, 0, 2)
    merged_values = jnp.concatenate([stored_values, fresh_values], 0).reshape(total_key_length, KEY_VALUE_HEADS, HEAD_SIZE).transpose(1, 0, 2)
    key_index = jnp.arange(total_key_length, dtype=jnp.int32)
    shard_of = jnp.minimum(key_index // CACHE_DEV, N_CTX - 1).astype(jnp.int32)
    offset_of = key_index % CACHE_DEV
    cache_ok = offset_of < jnp.take(cache_lengths, shard_of)
    is_cache = key_index < CACHED_POSITIONS
    new_pos = key_index - CACHED_POSITIONS
    grouped_queries = queries.reshape(NEW_TOKEN_COUNT, KEY_VALUE_HEADS, group_count, HEAD_SIZE).transpose(1, 2, 0, 3)
    block = math.gcd(NEW_TOKEN_COUNT, 512)
    block_count = NEW_TOKEN_COUNT // block

    def per_head(operands):
        head_q, head_k, head_v = operands
        key_f = head_k.astype(jnp.float32)
        value_f = head_v.astype(jnp.float32)

        def per_block(index):
            first_row = (index * block).astype(jnp.int32)
            query_block = lax.dynamic_slice_in_dim(head_q, first_row, block, 1).astype(jnp.float32)
            query_pos = first_row + jnp.arange(block, dtype=jnp.int32)
            allowed = jnp.where(is_cache[None, :], cache_ok[None, :], new_pos[None, :] <= query_pos[:, None])
            scores = jnp.einsum('gqd,kd->gqk', query_block, key_f) * score_scale
            masked = jnp.where(allowed[None], scores, -1e+30)
            row_max = lax.optimization_barrier(jnp.max(masked, axis=2, keepdims=True))
            weights = jnp.where(allowed[None], jnp.exp(masked - row_max), 0.0)
            row_total = lax.optimization_barrier(jnp.sum(weights, axis=2))
            probs = lax.optimization_barrier(weights.astype(jnp.bfloat16)).astype(jnp.float32)
            numer = jnp.einsum('gqk,kd->gqd', probs, value_f)
            return (numer / row_total[..., None]).astype(jnp.bfloat16)
        blocks = lax.map(per_block, jnp.arange(block_count, dtype=jnp.int32))
        return blocks.transpose(1, 0, 2, 3).reshape(group_count, NEW_TOKEN_COUNT, HEAD_SIZE)
    heads = lax.map(per_head, (grouped_queries, merged_keys, merged_values))
    attended = heads.transpose(2, 0, 1, 3).reshape(NEW_TOKEN_COUNT, QUERY_HEADS * HEAD_SIZE)
    return jnp.dot(attended, out_weight, preferred_element_type=jnp.float32).astype(jnp.bfloat16)
```

```python
import functools
import math

import jax
import jax.numpy as jnp
from jax import lax
from jax.experimental import pallas as pl
from jax.experimental.pallas import tpu as pltpu
from jax.sharding import PartitionSpec as P

HEAD = 128
NZ, NY, NC, NX, NL = 8, 2, 2, 4, 2
NEG = -1e30
VMEM = 48 * 1024 * 1024
F32 = jnp.float32
BF16 = jnp.bfloat16


def permute(value, move):
    pairs = []
    for z in range(NZ):
        for yh in range(NY):
            for c in range(NC):
                for x in range(NX):
                    for yl in range(NL):
                        z2, yh2, c2, x2, yl2 = move(z, yh, c, x, yl)
                        source = ((z * NY + yh) * NC + c) * NX * NL + x * NL + yl
                        target = (((z2 % NZ) * NY + yh2) * NC + c2) * NX * NL + (x2 % NX) * NL + yl2
                        pairs.append((source, target))
    return lax.ppermute(value, ("ctx", "tp"), pairs)


def shift_z(value, step):
    return permute(value, lambda z, yh, c, x, yl: (z + step, yh, c, x, yl))


def shift_x(value, step):
    return permute(value, lambda z, yh, c, x, yl: (z, yh, c, x + step, yl))


def swap(value, a=0, b=0, d=0):
    return permute(value, lambda z, yh, c, x, yl: (z, yh ^ a, c ^ b, x, yl ^ d))


def transpose_home(value, a):
    return permute(
        value, lambda z, yh, c, x, yl: (x * NL + yl, yh ^ a, c, z // NL, z % NL)
    )


def attend_kernel(shifts, first, last, rows, cache, fresh, meta, lens, q_ref, *refs):
    count = 2 * len(shifts)
    kv_refs, refs = refs[:count], refs[count:]
    if not first:
        acc_in, ml_in = refs[:2]
        refs = refs[2:]
    if last:
        keep_ref, send_ref, keep_lse, send_lse = refs
    else:
        acc_out, ml_out = refs
    z, yh, core = meta[0], meta[1], meta[2]
    factor = math.log2(math.e) / math.sqrt(HEAD)
    span = cache + fresh
    col = lax.broadcasted_iota(jnp.int32, (1, span), 1)
    step = min(256, rows)
    outs, lses = [], []
    for start in range(0, rows, step):
        q = q_ref[start : start + step, :]
        if first:
            m = jnp.full((step, 1), NEG, F32)
            l = jnp.zeros((step, 1), F32)
            acc = jnp.zeros((step, HEAD), F32)
        else:
            m = ml_in[start : start + step, 0:1]
            l = ml_in[start : start + step, 64:65]
            acc = acc_in[start : start + step, :]
        for index, shift in enumerate(shifts):
            zs = lax.rem(z + shift + NZ, NZ)
            parts = []
            for other in range(2):
                kv_ref = kv_refs[2 * index + other]
                block = yh * NC + (core if other == 0 else 1 - core)
                limit = lens[zs * NY * NC + block]
                s = lax.dot_general(
                    q, kv_ref[:, :HEAD], (((1,), (1,)), ((), ())), preferred_element_type=F32
                )
                if shift == 0:
                    row = start + lax.broadcasted_iota(jnp.int32, (step, span), 0)
                    cols = lax.broadcasted_iota(jnp.int32, (step, span), 1)
                    top = jnp.where(cols < cache, limit - 1, row + (cache - block * fresh))
                    s = jnp.where(cols <= top, s, NEG)
                else:
                    bound = jnp.where(zs < z, span, 0)
                    s = s + jnp.where(col < jnp.where(col < cache, limit, bound), 0.0, NEG)
                parts.append(s)
            top = jnp.maximum(parts[0], parts[1]).max(axis=1, keepdims=True)
            new = jnp.maximum(m, top)
            alpha = jnp.exp2((m - new) * factor)
            l = l * alpha
            acc = acc * alpha
            for other in range(2):
                p = jnp.exp2((parts[other] - new) * factor)
                l = l + p.sum(axis=1, keepdims=True)
                acc = acc + jnp.dot(
                    p.astype(BF16), kv_refs[2 * index + other][:, HEAD:], preferred_element_type=F32
                )
            m = new
        if last:
            outs.append((acc / l).astype(BF16))
            lses.append(jnp.broadcast_to(m * factor + jnp.log2(l), (step, HEAD)).T)
        else:
            acc_out[start : start + step, :] = acc
            lane = lax.broadcasted_iota(jnp.int32, (step, HEAD), 1)
            ml_out[start : start + step, :] = jnp.where(lane < 64, m, l)
    if last:
        out = jnp.concatenate(outs, 0)
        lse = jnp.concatenate(lses, 1)[0:8, :]

        @pl.when(pl.program_id(0) < 2)
        def _():
            keep_ref[...] = out
            keep_lse[0] = lse

        @pl.when(pl.program_id(0) >= 2)
        def _():
            send_ref[...] = out
            send_lse[0] = lse


def attend(meta, lens, q, kvs, shifts, state, last, cache, fresh):
    rows, width = q.shape
    heads = width // HEAD
    first = state is None
    span = cache + fresh
    whole = pl.BlockSpec((span, 2 * HEAD), lambda h, *_: (0, 0))
    per_head = pl.BlockSpec((rows, HEAD), lambda h, *_: (0, h))
    in_specs = [per_head] + [whole] * len(kvs)
    args = [q] + list(kvs)
    if not first:
        in_specs += [per_head, per_head]
        args += list(state)
    if last:
        half = heads // 2
        low = lambda h, *_: jnp.minimum(h, half - 1)
        high = lambda h, *_: jnp.maximum(h - half, 0)
        out_specs = [
            pl.BlockSpec((rows, HEAD), lambda h, *_: (0, low(h))),
            pl.BlockSpec((rows, HEAD), lambda h, *_: (0, high(h))),
            pl.BlockSpec((1, 8, rows), lambda h, *_: (low(h), 0, 0)),
            pl.BlockSpec((1, 8, rows), lambda h, *_: (high(h), 0, 0)),
        ]
        out_shape = [jax.ShapeDtypeStruct((rows, half * HEAD), BF16)] * 2
        out_shape += [jax.ShapeDtypeStruct((half, 8, rows), F32)] * 2
    else:
        out_specs = [per_head, per_head]
        out_shape = [jax.ShapeDtypeStruct((rows, width), F32)] * 2
    return pl.pallas_call(
        functools.partial(attend_kernel, tuple(shifts), first, last, rows, cache, fresh),
        grid_spec=pltpu.PrefetchScalarGridSpec(
            num_scalar_prefetch=2, grid=(heads,), in_specs=in_specs, out_specs=out_specs
        ),
        out_shape=out_shape,
        compiler_params=pltpu.CompilerParams(vmem_limit_bytes=VMEM),
        cost_estimate=pl.CostEstimate(
            flops=8 * rows * heads * HEAD * span * len(kvs),
            bytes_accessed=4 * rows * width,
            transcendentals=rows * heads * span * len(kvs),
        ),
    )(meta, lens, *args)


def combine_kernel(o0, l0, o1, l1, out):
    rows = o0.shape[0]
    wide = lambda ref: jnp.broadcast_to(ref[0, 0:1, :], (HEAD, rows)).T
    a, b = wide(l0), wide(l1)
    top = jnp.maximum(a, b)
    wa, wb = jnp.exp2(a - top), jnp.exp2(b - top)
    total = wa + wb
    out[...] = (
        (o0[...].astype(F32) * wa + o1[...].astype(F32) * wb) / total
    ).astype(BF16)


def combine(o0, l0, o1, l1):
    rows, width = o0.shape
    block = pl.BlockSpec((rows, HEAD), lambda h: (0, h))
    stat = pl.BlockSpec((1, 8, rows), lambda h: (h, 0, 0))
    return pl.pallas_call(
        combine_kernel,
        grid=(width // HEAD,),
        in_specs=[block, stat, block, stat],
        out_specs=block,
        out_shape=jax.ShapeDtypeStruct((rows, width), BF16),
        compiler_params=pltpu.CompilerParams(vmem_limit_bytes=VMEM),
    )(o0, l0, o1, l1)


def project_kernel(count, first, last, index, *refs):
    blocks, weights, refs = refs[:count], refs[count : 2 * count], refs[2 * count :]
    total = None
    if not first:
        total = refs[0][...]
        refs = refs[1:]
    for block, weight in zip(blocks, weights):
        term = jnp.dot(block[...], weight[0], preferred_element_type=F32)
        total = term if total is None else total + term
    if last:
        keep, send = refs

        @pl.when(pl.program_id(0) < 2)
        def _():
            keep[...] = total

        @pl.when(pl.program_id(0) >= 2)
        def _():
            send[...] = total.astype(BF16)
    else:
        refs[0][...] = total


def project(index, blocks, weight, total, last):
    rows, depth = blocks[0].shape
    width = weight.shape[2]
    tiles = 4
    tile = width // tiles
    count = len(blocks)
    first = total is None
    in_specs = [pl.BlockSpec((rows, depth), lambda j, idx: (0, 0))] * count
    for at in range(count):
        in_specs.append(
            pl.BlockSpec((1, depth, tile), functools.partial(lambda at, j, idx: (idx[at], 0, j), at))
        )
    args = list(blocks) + [weight] * count
    tiled = pl.BlockSpec((rows, tile), lambda j, idx: (0, j))
    if not first:
        in_specs.append(tiled)
        args.append(total)
    if last:
        out_specs = [
            pl.BlockSpec((rows, tile), lambda j, idx: (0, jnp.minimum(j, 1))),
            pl.BlockSpec((rows, tile), lambda j, idx: (0, jnp.maximum(j - 2, 0))),
        ]
        out_shape = [
            jax.ShapeDtypeStruct((rows, width // 2), F32),
            jax.ShapeDtypeStruct((rows, width // 2), BF16),
        ]
    else:
        out_specs = tiled
        out_shape = jax.ShapeDtypeStruct((rows, width), F32)
    return pl.pallas_call(
        functools.partial(project_kernel, count, first, last),
        grid_spec=pltpu.PrefetchScalarGridSpec(
            num_scalar_prefetch=1, grid=(tiles,), in_specs=in_specs, out_specs=out_specs
        ),
        out_shape=out_shape,
        compiler_params=pltpu.CompilerParams(vmem_limit_bytes=VMEM),
        cost_estimate=pl.CostEstimate(
            flops=2 * rows * depth * width * count,
            bytes_accessed=8 * rows * width,
            transcendentals=0,
        ),
    )(index, *args)


def shards(queries, stored_keys, stored_values, fresh_keys, fresh_values, cache_lengths, out_weight):
    cache, fresh = stored_keys.shape[0], fresh_keys.shape[0]
    ctx, tp = lax.axis_index("ctx"), lax.axis_index("tp")
    z, yh, core = ctx // (NY * NC), (ctx // NC) % NY, ctx % NC
    x, yl = tp // NL, tp % NL
    meta = jnp.stack([z, yh, core]).astype(jnp.int32)

    kv = jnp.concatenate(
        [
            jnp.concatenate([stored_keys, stored_values], 1),
            jnp.concatenate([fresh_keys, fresh_values], 1),
        ],
        0,
    )
    forth, back = [kv], [kv]
    for _ in range(3):
        forth.append(shift_z(forth[-1], 1))
        back.append(shift_z(back[-1], -1))
    forth.append(shift_z(forth[-1], 1))
    pair = lambda value: [value, swap(value, b=1)]

    half = queries.shape[1] // 2
    quarter = half // 2
    mine = lax.dynamic_slice_in_dim(queries, core * half, half, 1)
    theirs = lax.dynamic_slice_in_dim(queries, (1 - core) * half, half, 1)
    received = swap(theirs, b=1)
    near = jnp.where(
        core == 0,
        jnp.concatenate([mine, received], 0),
        jnp.concatenate([received, mine], 0),
    )
    far = swap(near, a=1)
    q = jnp.where(yh == 0, jnp.concatenate([near, far], 0), jnp.concatenate([far, near], 0))
    q = jnp.where(
        yh == 0, q, jnp.concatenate([q[:, quarter:], q[:, :quarter]], 1)
    )

    state = attend(
        meta, cache_lengths, q, pair(kv) + pair(forth[1]) + pair(back[1]), (0, -1, 1), None, False, cache, fresh
    )
    for step in (2, 3):
        state = attend(
            meta, cache_lengths, q, pair(forth[step]) + pair(back[step]), (-step, step), state, False, cache, fresh
        )
    keep, send, keep_lse, send_lse = attend(
        meta, cache_lengths, q, pair(forth[4]), (-4,), state, True, cache, fresh
    )

    depth = out_weight.shape[0] // 4

    def rows_of(a, b):
        return lax.dynamic_slice_in_dim(out_weight, ((core ^ b) * 2 + (yh ^ a)) * depth, depth, 0)

    own = jnp.concatenate(
        [rows_of(0, 0), swap(rows_of(1, 0), a=1), swap(rows_of(0, 1), b=1), swap(rows_of(1, 1), a=1, b=1)], 1
    )
    twin = swap(own, d=1)
    own_f, twin_f = shift_x(own, 1), shift_x(twin, 1)
    own_b, twin_b = shift_x(own, -1), shift_x(twin, -1)
    own_2, twin_2 = shift_x(own_f, 1), shift_x(twin_b, -1)
    weight = jnp.stack([own, twin, own_b, twin_b, own_2, twin_2, own_f, twin_f])

    def place(shift):
        group = (z + shift + NZ) % NZ
        return ((group // NL - x) % NX) * NL + (group % NL) ^ yl

    a = combine(
        transpose_home(keep, 0),
        transpose_home(keep_lse, 0),
        transpose_home(send, 1),
        transpose_home(send_lse, 1),
    )
    forth, back = [a], [a]
    for _ in range(3):
        forth.append(shift_z(forth[-1], 1))
        back.append(shift_z(back[-1], -1))
    forth.append(shift_z(forth[-1], 1))
    places = lambda *steps: jnp.stack([place(step) for step in steps]).astype(jnp.int32)
    total = project(places(0, -1, 1), [a, forth[1], back[1]], weight, None, False)
    total = project(places(-2, 2), [forth[2], back[2]], weight, total, False)
    total = project(places(-3, 3), [forth[3], back[3]], weight, total, False)
    kept, sent = project(places(-4), [forth[4]], weight, total, True)

    received = swap(sent, b=1)
    width = kept.shape[1] // 2
    part = (kept[:, width:] + received[:, width:].astype(F32)).astype(BF16)
    far = swap(part, a=1)
    return (kept[:, :width] + received[:, :width].astype(F32) + far.astype(F32)).astype(BF16)


def solution(mesh):
    return jax.shard_map(
        shards,
        mesh=mesh,
        in_specs=(
            P("ctx", "tp"),
            P("ctx", "tp"),
            P("ctx", "tp"),
            P("ctx", "tp"),
            P("ctx", "tp"),
            P(),
            P("tp", "ctx"),
        ),
        out_specs=P("tp", "ctx"),
        check_vma=False,
    )
```

```python
import functools
import math

import jax
import jax.numpy as jnp
from jax import lax
from jax.experimental import pallas as pl
from jax.experimental.pallas import tpu as pltpu
from jax.sharding import Mesh
from jax.sharding import PartitionSpec as P

HEAD = 128
NZ, NY, NC, NX, NL = 8, 2, 2, 4, 2
NEG = -1e30
VMEM = 48 * 1024 * 1024
AXES = ("z", "yh", "core", "x", "yl")
TILE = 256
TAIL = 16
F32 = jnp.float32
BF16 = jnp.bfloat16


def permute(value, move):
    pairs = []
    for z in range(NZ):
        for yh in range(NY):
            for c in range(NC):
                for x in range(NX):
                    for yl in range(NL):
                        z2, yh2, c2, x2, yl2 = move(z, yh, c, x, yl)
                        source = ((z * NY + yh) * NC + c) * NX * NL + x * NL + yl
                        target = (((z2 % NZ) * NY + yh2) * NC + c2) * NX * NL + (x2 % NX) * NL + yl2
                        pairs.append((source, target))
    return lax.ppermute(value, AXES, pairs)


def shift_z(value, step):
    return permute(value, lambda z, yh, c, x, yl: (z + step, yh, c, x, yl))


def shift_x(value, step):
    return permute(value, lambda z, yh, c, x, yl: (z, yh, c, x + step, yl))


def swap(value, a=0, b=0, d=0):
    return permute(value, lambda z, yh, c, x, yl: (z, yh ^ a, c ^ b, x, yl ^ d))


def attend_kernel(shifts, first, last, rows, cache, fresh, meta, lens, q_ref, *refs):
    count = 2 * len(shifts)
    kv_refs, refs = refs[:count], refs[count:]
    if not first:
        acc_in, ml_in = refs[:2]
        refs = refs[2:]
    z, yh, core = meta[0], meta[1], meta[2]
    factor = math.log2(math.e) / math.sqrt(HEAD)
    group = rows // NZ
    strip = group // (NY * NC)
    for start in range(0, rows, TILE):
        q = q_ref[start : start + TILE, :]
        row = start + lax.broadcasted_iota(jnp.int32, (TILE, 1), 0)
        place = (row // group) * (NY * NC * fresh) + ((row % group) // strip) * fresh + z * strip + row % strip
        parts, top = [], None
        for index in range(count):
            zs = lax.rem(z + shifts[index // 2] + NZ, NZ)
            block = zs * NY * NC + yh * NC + (core if index % 2 == 0 else 1 - core)
            s = lax.dot_general(
                q, kv_refs[index][:, :HEAD], (((1,), (1,)), ((), ())), preferred_element_type=F32
            )
            col = lax.broadcasted_iota(jnp.int32, (1, cache), 1)
            stored = s[:, :cache] + jnp.where(col < lens[block], 0.0, NEG)
            col = lax.broadcasted_iota(jnp.int32, (1, fresh), 1)
            new = jnp.where(block * fresh + col <= place, s[:, cache:], NEG)
            s = jnp.concatenate([stored, new], 1)
            parts.append(s)
            for at in range(0, cache + fresh, HEAD):
                piece = s[:, at : at + HEAD]
                top = piece if top is None else jnp.maximum(top, piece)
        m = top.max(axis=1, keepdims=True)
        if first:
            l, acc = 0.0, 0.0
        else:
            before = ml_in[start : start + TILE, 0:1]
            m = jnp.maximum(m, before)
            alpha = jnp.exp2((before - m) * factor)
            l = ml_in[start : start + TILE, 64:65] * alpha
            acc = acc_in[start : start + TILE, :] * alpha
        for index in range(count):
            p = jnp.exp2((parts[index] - m) * factor)
            l = l + p.sum(axis=1, keepdims=True)
            acc = acc + jnp.dot(p.astype(BF16), kv_refs[index][:, HEAD:], preferred_element_type=F32)
        if not last:
            acc_out, ml_out = refs
            acc_out[start : start + TILE, :] = acc
            lane = lax.broadcasted_iota(jnp.int32, (TILE, HEAD), 1)
            ml_out[start : start + TILE, :] = jnp.where(lane < 64, m, l)
            continue
        out_ref = refs[0]
        out = (acc / l).astype(BF16)
        lse = m * factor + jnp.log2(l)
        for at in range(0, TILE, group):
            out_ref[0, (start + at) // group, 0:group, :] = out[at : at + group, :]
        for at in range(0, TILE, 2 * group):
            line = jnp.broadcast_to(lse[at : at + 2 * group, :], (2 * group, HEAD)).T[0:1, :]
            high = line.astype(BF16).astype(F32)
            middle = (line - high).astype(BF16).astype(F32)
            low = line - high - middle
            which = lax.broadcasted_iota(jnp.int32, (TAIL, HEAD), 0)
            tail = jnp.where(which == 0, high, jnp.where(which == 1, middle, low)).astype(BF16)
            for half in range(2):
                out_ref[0, (start + at) // group + half, group : group + TAIL, :] = tail


def attend(meta, lens, q, kvs, shifts, state, last, cache, fresh):
    rows, width = q.shape
    heads = width // HEAD
    group = rows // NZ
    first = state is None
    span = cache + fresh
    whole = pl.BlockSpec((span, 2 * HEAD), lambda h, *_: (0, 0))
    per_head = pl.BlockSpec((rows, HEAD), lambda h, *_: (0, h))
    in_specs = [per_head] + [whole] * len(kvs)
    args = [q] + list(kvs)
    if not first:
        in_specs += [per_head, per_head]
        args += list(state)
    if last:
        pair = heads // NY
        out_specs = pl.BlockSpec((1, NZ, group + TAIL, HEAD), lambda h, *_: (h // pair, 0, 0, h % pair))
        out_shape = jax.ShapeDtypeStruct((NY, NZ, group + TAIL, pair * HEAD), BF16)
    else:
        out_specs = [per_head, per_head]
        out_shape = [jax.ShapeDtypeStruct((rows, width), F32)] * 2
    return pl.pallas_call(
        functools.partial(attend_kernel, tuple(shifts), first, last, rows, cache, fresh),
        grid_spec=pltpu.PrefetchScalarGridSpec(
            num_scalar_prefetch=2, grid=(heads,), in_specs=in_specs, out_specs=out_specs
        ),
        out_shape=out_shape,
        compiler_params=pltpu.CompilerParams(vmem_limit_bytes=VMEM),
        cost_estimate=pl.CostEstimate(
            flops=8 * rows * heads * HEAD * span * len(kvs),
            bytes_accessed=4 * rows * width,
            transcendentals=rows * heads * span * len(kvs),
        ),
    )(meta, lens, *args)


def combine_kernel(group, meta, pieces, out):
    x, yl = meta[3], meta[4]

    def one(t, _):
        spot = lax.rem(t // NL - x + NX, NX) * NL + lax.rem(t + yl, NL)
        for at in range(0, pieces.shape[2], HEAD):
            values, weights = [], []
            for half in range(NY):
                tail = pieces[half * NX * NL + t, group:, at : at + HEAD].astype(F32)
                line = tail[0:1, :] + tail[1:2, :] + tail[2:3, :]
                wide = jnp.broadcast_to(line, (HEAD, HEAD)).T
                weights.append(jnp.where(yl == 0, wide[:group, :], wide[group : 2 * group, :]))
                values.append(pieces[half * NX * NL + t, 0:group, at : at + HEAD].astype(F32))
            top = jnp.maximum(weights[0], weights[1])
            a, b = jnp.exp2(weights[0] - top), jnp.exp2(weights[1] - top)
            joined = (values[0] * a + values[1] * b) / (a + b)
            out[:, pl.ds(pl.multiple_of(spot * pieces.shape[2] + at, HEAD), HEAD)] = joined.astype(BF16)
        return 0

    lax.fori_loop(0, NX * NL, one, 0, unroll=True)


def combine(meta, pieces):
    group, width = pieces.shape[1] - TAIL, pieces.shape[2]
    return pl.pallas_call(
        functools.partial(combine_kernel, group),
        in_specs=[pl.BlockSpec(memory_space=pltpu.SMEM), pl.BlockSpec(memory_space=pltpu.VMEM)],
        out_specs=pl.BlockSpec(memory_space=pltpu.VMEM),
        out_shape=jax.ShapeDtypeStruct((group, NX * NL * width), BF16),
        compiler_params=pltpu.CompilerParams(vmem_limit_bytes=VMEM),
    )(meta, pieces)


def project_kernel(count, *refs):
    blocks, weights, (keep, send) = refs[:count], refs[count:-2], refs[-2:]
    depth = weights[0].shape[0]
    total = None
    for at, weight in enumerate(weights):
        a = jnp.concatenate([block[:, at * depth : (at + 1) * depth] for block in blocks], 0)
        term = jnp.dot(a, weight[...], preferred_element_type=F32)
        total = term if total is None else total + term

    @pl.when(pl.program_id(0) < 2)
    def _():
        keep[...] = total

    @pl.when(pl.program_id(0) >= 2)
    def _():
        send[...] = total.astype(BF16)


def project(blocks, weights):
    rows = blocks[0].shape[0] * len(blocks)
    depth, width = weights[0].shape
    tile = width // 4
    whole = pl.BlockSpec(blocks[0].shape, lambda j: (0, 0))
    column = pl.BlockSpec((depth, tile), lambda j: (0, j))
    return pl.pallas_call(
        functools.partial(project_kernel, len(blocks)),
        grid=(4,),
        in_specs=[whole] * len(blocks) + [column] * len(weights),
        out_specs=[
            pl.BlockSpec((rows, tile), lambda j: (0, jnp.minimum(j, 1))),
            pl.BlockSpec((rows, tile), lambda j: (0, jnp.maximum(j - 2, 0))),
        ],
        out_shape=[
            jax.ShapeDtypeStruct((rows, width // 2), F32),
            jax.ShapeDtypeStruct((rows, width // 2), BF16),
        ],
        compiler_params=pltpu.CompilerParams(vmem_limit_bytes=VMEM),
        cost_estimate=pl.CostEstimate(
            flops=2 * rows * depth * width * len(weights),
            bytes_accessed=8 * depth * width,
            transcendentals=0,
        ),
    )(*blocks, *weights)


def finish_kernel(order, strip, meta, *refs):
    out = refs[-1]
    width = out.shape[1]
    z = meta[0]
    parts = len(order)
    for part, shifts in enumerate(order):
        kept, core, far = refs[3 * part : 3 * part + 3]
        for at, shift in enumerate(shifts):
            zs = lax.rem(z + shift + NZ, NZ)
            for p in range(NY * NC):
                here = pl.ds((at * NY * NC + p) * strip, strip)
                total = kept[here, :width] + core[here, :width].astype(F32) + far[here, :].astype(F32)
                spot = pl.multiple_of((p * NZ + zs) * strip, strip)
                out[pl.ds(spot, strip), :] = total.astype(BF16)


def finish(meta, order, parts):
    strip = 16
    rows = sum(part[0].shape[0] for part in parts)
    flat = [array for part in parts for array in part]
    return pl.pallas_call(
        functools.partial(finish_kernel, order, strip),
        in_specs=[pl.BlockSpec(memory_space=pltpu.SMEM)] + [pl.BlockSpec(memory_space=pltpu.VMEM)] * len(flat),
        out_specs=pl.BlockSpec(memory_space=pltpu.VMEM),
        out_shape=jax.ShapeDtypeStruct((rows, parts[0][2].shape[1]), BF16),
        compiler_params=pltpu.CompilerParams(vmem_limit_bytes=VMEM),
    )(meta, *flat)


def shards(queries, stored_keys, stored_values, fresh_keys, fresh_values, cache_lengths, out_weight):
    cache, fresh = stored_keys.shape[0], fresh_keys.shape[0]
    z, yh, core, x, yl = [lax.axis_index(name) for name in AXES]
    meta = jnp.stack([z, yh, core, x, yl]).astype(jnp.int32)

    kv = jnp.concatenate(
        [
            jnp.concatenate([stored_keys, stored_values], 1),
            jnp.concatenate([fresh_keys, fresh_values], 1),
        ],
        0,
    )
    forth, back = [kv], [kv]
    for _ in range(3):
        forth.append(shift_z(forth[-1], 1))
        back.append(shift_z(back[-1], -1))
    forth.append(shift_z(forth[-1], 1))
    pair = lambda value: [value, swap(value, b=1)]

    half = queries.shape[1] // 2
    mine = lax.dynamic_slice_in_dim(queries, core * half, half, 1)
    theirs = lax.dynamic_slice_in_dim(queries, (1 - core) * half, half, 1)
    received = swap(theirs, b=1)
    strips = lambda value: value.reshape(NZ, 1, fresh // NZ, half)
    near = jnp.where(
        core == 0,
        jnp.concatenate([strips(mine), strips(received)], 1),
        jnp.concatenate([strips(received), strips(mine)], 1),
    )
    near = jnp.broadcast_to(near[:, None], (NZ, NY, NC, fresh // NZ, half))
    q = lax.all_to_all(
        near.reshape(NZ * NY, NC * fresh // NZ, half), ("z", "yh"), split_axis=0, concat_axis=0, tiled=True
    ).reshape(NY * NC * fresh, half)

    state = attend(
        meta, cache_lengths, q, pair(kv) + pair(forth[1]) + pair(back[1]), (0, -1, 1), None, False, cache, fresh
    )
    state = attend(
        meta, cache_lengths, q, pair(forth[2]) + pair(back[2]), (-2, 2), state, False, cache, fresh
    )
    state = attend(
        meta, cache_lengths, q, pair(forth[3]) + pair(back[3]), (-3, 3), state, False, cache, fresh
    )
    pieces = attend(meta, cache_lengths, q, pair(forth[4]), (-4,), state, True, cache, fresh)

    depth = out_weight.shape[0] // 4

    def rows_of(a, b):
        return lax.dynamic_slice_in_dim(out_weight, ((core ^ b) * 2 + (yh ^ a)) * depth, depth, 0)

    own = jnp.concatenate(
        [rows_of(0, 0), swap(rows_of(1, 0), a=1), swap(rows_of(0, 1), b=1), swap(rows_of(1, 1), a=1, b=1)], 1
    )
    twin = swap(own, d=1)
    own_f, twin_f = shift_x(own, 1), shift_x(twin, 1)
    own_b, twin_b = shift_x(own, -1), shift_x(twin, -1)
    own_2, twin_2 = shift_x(own_f, 1), shift_x(twin_b, -1)
    weights = [own, twin, own_b, twin_b, own_2, twin_2, own_f, twin_f]

    group, width = pieces.shape[2] , pieces.shape[3]
    pieces = lax.all_to_all(
        pieces.reshape(NY * NZ, group, width), ("yh", "x", "yl"), split_axis=0, concat_axis=0, tiled=True
    )
    a = combine(meta, pieces)
    forth, back = [a], [a]
    for _ in range(3):
        forth.append(shift_z(forth[-1], 1))
        back.append(shift_z(back[-1], -1))
    forth.append(shift_z(forth[-1], 1))

    def share(blocks):
        kept, sent = project(blocks, weights)
        near = swap(sent, b=1)
        width = kept.shape[1] // 2
        part = (kept[:, width:] + near[:, width:].astype(F32)).astype(BF16)
        return kept, near, swap(part, a=1)

    order = ((0, -1, 1, -2, 2), (-3, 3, -4))
    first = share([a, forth[1], back[1], forth[2], back[2]])
    second = share([forth[3], back[3], forth[4]])
    return finish(meta, order, (first, second))


def solution(mesh):
    split = Mesh(mesh.devices.reshape(NZ, NY, NC, NX, NL), AXES)
    ctx, tp = ("z", "yh", "core"), ("x", "yl")
    spec = P(ctx, tp)
    return jax.shard_map(
        shards,
        mesh=split,
        in_specs=(spec, spec, spec, spec, spec, P(), P(tp, ctx)),
        out_specs=P(tp, ctx),
        check_vma=False,
    )
```

```python
import functools
import math

import jax
import jax.numpy as jnp
from jax import lax
from jax.experimental import pallas as pl
from jax.experimental.pallas import tpu as pltpu
from jax.sharding import Mesh
from jax.sharding import PartitionSpec as P

HEAD = 128
NZ, NY, NC, NX, NL = 8, 2, 2, 4, 2
NEG = -1e30
VMEM = 48 * 1024 * 1024
AXES = ("z", "yh", "core", "x", "yl")
TILE = 512
TAIL = 16
F32 = jnp.float32
BF16 = jnp.bfloat16


def permute(value, move):
    pairs = []
    for z in range(NZ):
        for yh in range(NY):
            for c in range(NC):
                for x in range(NX):
                    for yl in range(NL):
                        z2, yh2, c2, x2, yl2 = move(z, yh, c, x, yl)
                        source = ((z * NY + yh) * NC + c) * NX * NL + x * NL + yl
                        target = (((z2 % NZ) * NY + yh2) * NC + c2) * NX * NL + (x2 % NX) * NL + yl2
                        pairs.append((source, target))
    return lax.ppermute(value, AXES, pairs)


def shift_z(value, step):
    return permute(value, lambda z, yh, c, x, yl: (z + step, yh, c, x, yl))


def shift_x(value, step):
    return permute(value, lambda z, yh, c, x, yl: (z, yh, c, x + step, yl))


def swap(value, a=0, b=0, d=0):
    return permute(value, lambda z, yh, c, x, yl: (z, yh ^ a, c ^ b, x, yl ^ d))


def attend_kernel(shifts, first, last, rows, cache, fresh, meta, lens, q_ref, *refs):
    count = 2 * len(shifts)
    kv_refs, refs = refs[:count], refs[count:]
    if not first:
        acc_in, top_in, sum_in = refs[:3]
        refs = refs[3:]
    z, yh, core = meta[0], meta[1], meta[2]
    factor = math.log2(math.e) / math.sqrt(HEAD)
    for start in range(0, rows, TILE):
        here = slice(start, start + TILE)
        q = q_ref[here, :]
        parts, top = [], None
        for index in range(count):
            shift = shifts[index // 2]
            zs = lax.rem(z + shift + NZ, NZ)
            mine = yh * NC + (core if index % 2 == 0 else 1 - core)
            s = lax.dot_general(
                q, kv_refs[index][:, :HEAD], (((1,), (1,)), ((), ())), preferred_element_type=F32
            )
            col = lax.broadcasted_iota(jnp.int32, (1, cache), 1)
            stored = s[:, :cache] + jnp.where(col < lens[zs * NY * NC + mine], 0.0, NEG)
            if shift == 0:
                row = start + lax.broadcasted_iota(jnp.int32, (TILE, fresh), 0)
                col = mine * fresh + lax.broadcasted_iota(jnp.int32, (TILE, fresh), 1)
                new = jnp.where(col <= row, s[:, cache:], NEG)
            else:
                new = s[:, cache:] + jnp.where(zs < z, 0.0, NEG)
            s = jnp.concatenate([stored, new], 1)
            parts.append(s)
            for at in range(0, cache + fresh, HEAD):
                piece = s[:, at : at + HEAD]
                top = piece if top is None else jnp.maximum(top, piece)
        m = top.max(axis=1, keepdims=True)
        if first:
            l, acc = None, None
        else:
            before = top_in[here, :]
            m = jnp.maximum(m, before)
            alpha = jnp.exp2((before - m) * factor)
            m = m[:, 0:1]
            l = sum_in[here, :] * alpha
            acc = acc_in[here, :] * alpha
        for index in range(count):
            p = jnp.exp2((parts[index] - m) * factor)
            for at in range(0, cache + fresh, HEAD):
                piece = p[:, at : at + HEAD]
                l = piece if l is None else l + piece
            term = jnp.dot(p.astype(BF16), kv_refs[index][:, HEAD:], preferred_element_type=F32)
            acc = term if acc is None else acc + term
        if not last:
            acc_out, top_out, sum_out = refs
            acc_out[here, :] = acc
            top_out[here, :] = jnp.broadcast_to(m, (TILE, HEAD))
            sum_out[here, :] = l
            continue
        out_ref = refs[0]
        l = l.sum(axis=1, keepdims=True)
        out = (acc / l).astype(BF16)
        lse = m * factor + jnp.log2(l)
        group = rows // (NX * NL)
        for at in range(0, TILE, group):
            out_ref[0, (start + at) // group, 0:group, :] = out[at : at + group, :]
        for at in range(0, TILE, 2 * group):
            line = jnp.broadcast_to(lse[at : at + 2 * group, :], (2 * group, HEAD)).T[0:1, :]
            high = line.astype(BF16).astype(F32)
            middle = (line - high).astype(BF16).astype(F32)
            low = line - high - middle
            which = lax.broadcasted_iota(jnp.int32, (TAIL, HEAD), 0)
            tail = jnp.where(which == 0, high, jnp.where(which == 1, middle, low)).astype(BF16)
            for half in range(2):
                out_ref[0, (start + at) // group + half, group : group + TAIL, :] = tail


def attend(meta, lens, q, kvs, shifts, state, last, cache, fresh):
    rows, width = q.shape
    heads = width // HEAD
    group = rows // (NX * NL)
    first = state is None
    span = cache + fresh
    whole = pl.BlockSpec((span, 2 * HEAD), lambda h, *_: (0, 0))
    per_head = pl.BlockSpec((rows, HEAD), lambda h, *_: (0, h))
    in_specs = [per_head] + [whole] * len(kvs)
    args = [q] + list(kvs)
    if not first:
        in_specs += [per_head] * 3
        args += list(state)
    if last:
        pair = heads // NY
        out_specs = pl.BlockSpec((1, NX * NL, group + TAIL, HEAD), lambda h, *_: (h // pair, 0, 0, h % pair))
        out_shape = jax.ShapeDtypeStruct((NY, NX * NL, group + TAIL, pair * HEAD), BF16)
    else:
        out_specs = [per_head] * 3
        out_shape = [jax.ShapeDtypeStruct((rows, width), F32)] * 3
    return pl.pallas_call(
        functools.partial(attend_kernel, tuple(shifts), first, last, rows, cache, fresh),
        grid_spec=pltpu.PrefetchScalarGridSpec(
            num_scalar_prefetch=2, grid=(heads,), in_specs=in_specs, out_specs=out_specs
        ),
        out_shape=out_shape,
        compiler_params=pltpu.CompilerParams(vmem_limit_bytes=VMEM),
        cost_estimate=pl.CostEstimate(
            flops=8 * rows * heads * HEAD * span * len(kvs),
            bytes_accessed=4 * rows * width,
            transcendentals=rows * heads * span * len(kvs),
        ),
    )(meta, lens, *args)


def combine_kernel(group, meta, pieces, out):
    x, yl = meta[3], meta[4]

    def one(t, _):
        spot = lax.rem(t // NL - x + NX, NX) * NL + lax.rem(t + yl, NL)
        for at in range(0, pieces.shape[2], HEAD):
            values, weights = [], []
            for half in range(NY):
                tail = pieces[half * NX * NL + t, group:, at : at + HEAD].astype(F32)
                line = tail[0:1, :] + tail[1:2, :] + tail[2:3, :]
                wide = jnp.broadcast_to(line, (HEAD, HEAD)).T
                weights.append(jnp.where(yl == 0, wide[:group, :], wide[group : 2 * group, :]))
                values.append(pieces[half * NX * NL + t, 0:group, at : at + HEAD].astype(F32))
            top = jnp.maximum(weights[0], weights[1])
            a, b = jnp.exp2(weights[0] - top), jnp.exp2(weights[1] - top)
            joined = (values[0] * a + values[1] * b) / (a + b)
            out[:, pl.ds(pl.multiple_of(spot * pieces.shape[2] + at, HEAD), HEAD)] = joined.astype(BF16)
        return 0

    lax.fori_loop(0, NX * NL, one, 0, unroll=True)


def combine(meta, pieces):
    group, width = pieces.shape[1] - TAIL, pieces.shape[2]
    return pl.pallas_call(
        functools.partial(combine_kernel, group),
        in_specs=[pl.BlockSpec(memory_space=pltpu.SMEM), pl.BlockSpec(memory_space=pltpu.VMEM)],
        out_specs=pl.BlockSpec(memory_space=pltpu.VMEM),
        out_shape=jax.ShapeDtypeStruct((group, NX * NL * width), BF16),
        compiler_params=pltpu.CompilerParams(vmem_limit_bytes=VMEM),
    )(meta, pieces)


def project_kernel(count, *refs):
    blocks, weights, (keep, send) = refs[:count], refs[count:-2], refs[-2:]
    depth = weights[0].shape[0]
    total = None
    for at, weight in enumerate(weights):
        a = jnp.concatenate([block[:, at * depth : (at + 1) * depth] for block in blocks], 0)
        term = jnp.dot(a, weight[...], preferred_element_type=F32)
        total = term if total is None else total + term

    @pl.when(pl.program_id(0) < 2)
    def _():
        keep[...] = total

    @pl.when(pl.program_id(0) >= 2)
    def _():
        send[...] = total.astype(BF16)


def project(blocks, weights):
    rows = blocks[0].shape[0] * len(blocks)
    depth, width = weights[0].shape
    tile = width // 4
    whole = pl.BlockSpec(blocks[0].shape, lambda j: (0, 0))
    column = pl.BlockSpec((depth, tile), lambda j: (0, j))
    return pl.pallas_call(
        functools.partial(project_kernel, len(blocks)),
        grid=(4,),
        in_specs=[whole] * len(blocks) + [column] * len(weights),
        out_specs=[
            pl.BlockSpec((rows, tile), lambda j: (0, jnp.minimum(j, 1))),
            pl.BlockSpec((rows, tile), lambda j: (0, jnp.maximum(j - 2, 0))),
        ],
        out_shape=[
            jax.ShapeDtypeStruct((rows, width // 2), F32),
            jax.ShapeDtypeStruct((rows, width // 2), BF16),
        ],
        compiler_params=pltpu.CompilerParams(vmem_limit_bytes=VMEM),
        cost_estimate=pl.CostEstimate(
            flops=2 * rows * depth * width * len(weights),
            bytes_accessed=8 * depth * width,
            transcendentals=0,
        ),
    )(*blocks, *weights)


def settle_kernel(order, meta, *refs):
    out = refs[-1]
    width = out.shape[3]
    z, yh = meta[0], meta[1]
    for part, shifts in enumerate(order):
        kept, near = refs[2 * part : 2 * part + 2]
        group = kept.shape[0] // len(shifts)
        for at, shift in enumerate(shifts):
            zs = lax.rem(z + shift + NZ, NZ)
            here = pl.ds(at * group, group)
            total = (kept[here, :] + near[here, :].astype(F32)).astype(BF16)
            for half in range(NY):
                out[lax.rem(yh + half, NY), zs] = total[:, half * width : (half + 1) * width]


def settle(meta, order, parts):
    rows = sum(part[0].shape[0] for part in parts)
    width = parts[0][0].shape[1] // NY
    flat = [array for part in parts for array in part]
    return pl.pallas_call(
        functools.partial(settle_kernel, order),
        in_specs=[pl.BlockSpec(memory_space=pltpu.SMEM)] + [pl.BlockSpec(memory_space=pltpu.VMEM)] * len(flat),
        out_specs=pl.BlockSpec(memory_space=pltpu.VMEM),
        out_shape=jax.ShapeDtypeStruct((NY, NZ, rows // NZ, width), BF16),
        compiler_params=pltpu.CompilerParams(vmem_limit_bytes=VMEM),
    )(meta, *flat)


def shards(queries, stored_keys, stored_values, fresh_keys, fresh_values, cache_lengths, out_weight):
    cache, fresh = stored_keys.shape[0], fresh_keys.shape[0]
    z, yh, core, x, yl = [lax.axis_index(name) for name in AXES]
    meta = jnp.stack([z, yh, core, x, yl]).astype(jnp.int32)

    kv = jnp.concatenate(
        [
            jnp.concatenate([stored_keys, stored_values], 1),
            jnp.concatenate([fresh_keys, fresh_values], 1),
        ],
        0,
    )
    forth, back = [kv], [kv]
    for _ in range(3):
        forth.append(shift_z(forth[-1], 1))
        back.append(shift_z(back[-1], -1))
    forth.append(shift_z(forth[-1], 1))
    pair = lambda value: [value, swap(value, b=1)]

    half = queries.shape[1] // 2
    mine = lax.dynamic_slice_in_dim(queries, core * half, half, 1)
    theirs = lax.dynamic_slice_in_dim(queries, (1 - core) * half, half, 1)
    received = swap(theirs, b=1)
    near = jnp.where(
        core == 0,
        jnp.concatenate([mine, received], 0),
        jnp.concatenate([received, mine], 0),
    )
    far = swap(near, a=1)
    q = jnp.where(yh == 0, jnp.concatenate([near, far], 0), jnp.concatenate([far, near], 0))

    near_kv = pair(kv) + pair(forth[1]) + pair(back[1]) + pair(forth[2]) + pair(back[2])
    state = attend(meta, cache_lengths, q, near_kv, (0, -1, 1, -2, 2), None, False, cache, fresh)
    far_kv = pair(forth[3]) + pair(back[3]) + pair(forth[4])
    pieces = attend(meta, cache_lengths, q, far_kv, (-3, 3, -4), state, True, cache, fresh)

    depth = out_weight.shape[0] // 4

    def rows_of(a, b):
        return lax.dynamic_slice_in_dim(out_weight, ((core ^ b) * 2 + (yh ^ a)) * depth, depth, 0)

    own = jnp.concatenate(
        [rows_of(0, 0), swap(rows_of(1, 0), a=1), swap(rows_of(0, 1), b=1), swap(rows_of(1, 1), a=1, b=1)], 1
    )
    twin = swap(own, d=1)
    own_f, twin_f = shift_x(own, 1), shift_x(twin, 1)
    own_b, twin_b = shift_x(own, -1), shift_x(twin, -1)
    own_2, twin_2 = shift_x(own_f, 1), shift_x(twin_b, -1)
    weights = [own, twin, own_b, twin_b, own_2, twin_2, own_f, twin_f]

    group, width = pieces.shape[2], pieces.shape[3]
    pieces, weights = lax.optimization_barrier((pieces, weights))
    pieces = lax.all_to_all(
        pieces.reshape(NY * NZ, group, width), ("yh", "x", "yl"), split_axis=0, concat_axis=0, tiled=True
    )
    a = combine(meta, pieces)
    forth, back = [a], [a]
    for _ in range(3):
        forth.append(shift_z(forth[-1], 1))
        back.append(shift_z(back[-1], -1))
    forth.append(shift_z(forth[-1], 1))

    def share(blocks):
        kept, sent = project(blocks, weights)
        return kept, swap(sent, b=1)

    order = ((0, -1, 1, -2, 2), (-3, 3, -4))
    first = share([a, forth[1], back[1], forth[2], back[2]])
    second = share([forth[3], back[3], forth[4]])
    settled = settle(meta, order, (first, second))
    rows, width = settled.shape[2:]
    home = lax.all_to_all(
        settled.reshape(NY * NZ, rows, width), ("yh", "x", "yl"), split_axis=0, concat_axis=0, tiled=True
    ).reshape(NY, NZ * rows, width)
    return (home[0].astype(F32) + home[1].astype(F32)).astype(BF16)


def solution(mesh):
    split = Mesh(mesh.devices.reshape(NZ, NY, NC, NX, NL), AXES)
    ctx, tp = ("z", "yh", "core"), ("x", "yl")
    spec = P(ctx, tp)
    return jax.shard_map(
        shards,
        mesh=split,
        in_specs=(spec, spec, spec, spec, spec, P(), P(tp, ctx)),
        out_specs=P(tp, ctx),
        check_vma=False,
    )
```

```python
import functools
import math

import jax
import jax.numpy as jnp
from jax import lax
from jax.experimental import pallas as pl
from jax.experimental.pallas import tpu as pltpu
from jax.sharding import Mesh
from jax.sharding import PartitionSpec as P

HEAD = 128
NZ, NY, NC, NX, NL = 8, 2, 2, 4, 2
NEG = -1e30
VMEM = 48 * 1024 * 1024
AXES = ("z", "yh", "core", "x", "yl")
TILE = 512
TAIL = 16
F32 = jnp.float32
BF16 = jnp.bfloat16


def permute(value, move):
    pairs = []
    for z in range(NZ):
        for yh in range(NY):
            for c in range(NC):
                for x in range(NX):
                    for yl in range(NL):
                        z2, yh2, c2, x2, yl2 = move(z, yh, c, x, yl)
                        source = ((z * NY + yh) * NC + c) * NX * NL + x * NL + yl
                        target = (((z2 % NZ) * NY + yh2) * NC + c2) * NX * NL + (x2 % NX) * NL + yl2
                        pairs.append((source, target))
    return lax.ppermute(value, AXES, pairs)


def shift_z(value, step):
    return permute(value, lambda z, yh, c, x, yl: (z + step, yh, c, x, yl))


def shift_x(value, step):
    return permute(value, lambda z, yh, c, x, yl: (z, yh, c, x + step, yl))


def swap(value, a=0, b=0, d=0):
    return permute(value, lambda z, yh, c, x, yl: (z, yh ^ a, c ^ b, x, yl ^ d))


def attend_kernel(sources, first, last, rows, cache, fresh, meta, lens, q_ref, *refs):
    count = len(sources)
    kv_refs, refs = refs[:count], refs[count:]
    if not first:
        acc_in, top_in, sum_in = refs[:3]
        refs = refs[3:]
    z, yh, core = meta[0], meta[1], meta[2]
    factor = math.log2(math.e) / math.sqrt(HEAD)
    for start in range(0, rows, TILE):
        here = slice(start, start + TILE)
        q = q_ref[here, :]
        parts, top = [], None
        for index in range(count):
            shift, other = sources[index]
            zs = lax.rem(z + shift + NZ, NZ)
            mine = yh * NC + (1 - core if other else core)
            s = lax.dot_general(
                q, kv_refs[index][:, :HEAD], (((1,), (1,)), ((), ())), preferred_element_type=F32
            )
            col = lax.broadcasted_iota(jnp.int32, (1, cache), 1)
            stored = s[:, :cache] + jnp.where(col < lens[zs * NY * NC + mine], 0.0, NEG)
            if shift == 0:
                row = start + lax.broadcasted_iota(jnp.int32, (TILE, fresh), 0)
                col = mine * fresh + lax.broadcasted_iota(jnp.int32, (TILE, fresh), 1)
                new = jnp.where(col <= row, s[:, cache:], NEG)
            else:
                new = s[:, cache:] + jnp.where(zs < z, 0.0, NEG)
            s = jnp.concatenate([stored, new], 1)
            parts.append(s)
            for at in range(0, cache + fresh, HEAD):
                piece = s[:, at : at + HEAD]
                top = piece if top is None else jnp.maximum(top, piece)
        m = top.max(axis=1, keepdims=True)
        if first:
            l, acc = None, None
        else:
            before = top_in[here, :]
            m = jnp.maximum(m, before)
            alpha = jnp.exp2((before - m) * factor)
            m = m[:, 0:1]
            l = sum_in[here, :] * alpha
            acc = acc_in[here, :] * alpha
        for index in range(count):
            p = jnp.exp2((parts[index] - m) * factor)
            for at in range(0, cache + fresh, HEAD):
                piece = p[:, at : at + HEAD]
                l = piece if l is None else l + piece
            term = jnp.dot(p.astype(BF16), kv_refs[index][:, HEAD:], preferred_element_type=F32)
            acc = term if acc is None else acc + term
        if not last:
            acc_out, top_out, sum_out = refs
            acc_out[here, :] = acc
            top_out[here, :] = jnp.broadcast_to(m, (TILE, HEAD))
            sum_out[here, :] = l
            continue
        out_ref = refs[0]
        l = l.sum(axis=1, keepdims=True)
        out = (acc / l).astype(BF16)
        lse = m * factor + jnp.log2(l)
        group = rows // (NX * NL)
        for at in range(0, TILE, group):
            out_ref[0, (start + at) // group, 0:group, :] = out[at : at + group, :]
        for at in range(0, TILE, 2 * group):
            line = jnp.broadcast_to(lse[at : at + 2 * group, :], (2 * group, HEAD)).T[0:1, :]
            high = line.astype(BF16).astype(F32)
            middle = (line - high).astype(BF16).astype(F32)
            low = line - high - middle
            which = lax.broadcasted_iota(jnp.int32, (TAIL, HEAD), 0)
            tail = jnp.where(which == 0, high, jnp.where(which == 1, middle, low)).astype(BF16)
            for half in range(2):
                out_ref[0, (start + at) // group + half, group : group + TAIL, :] = tail


def attend(meta, lens, q, kvs, state, last, cache, fresh):
    rows, width = q.shape
    heads = width // HEAD
    group = rows // (NX * NL)
    first = state is None
    span = cache + fresh
    whole = [
        pl.BlockSpec((span, 2 * HEAD), functools.partial(lambda at, h, *_: (at, 0), at)) for _, at, _, _ in kvs
    ]
    per_head = pl.BlockSpec((rows, HEAD), lambda h, *_: (0, h))
    in_specs = [per_head] + whole
    args = [q] + [entry[0] for entry in kvs]
    if not first:
        in_specs += [per_head] * 3
        args += list(state)
    if last:
        pair = heads // NY
        out_specs = pl.BlockSpec((1, NX * NL, group + TAIL, HEAD), lambda h, *_: (h // pair, 0, 0, h % pair))
        out_shape = jax.ShapeDtypeStruct((NY, NX * NL, group + TAIL, pair * HEAD), BF16)
    else:
        out_specs = [per_head] * 3
        out_shape = [jax.ShapeDtypeStruct((rows, width), F32)] * 3
    return pl.pallas_call(
        functools.partial(attend_kernel, tuple(entry[2:] for entry in kvs), first, last, rows, cache, fresh),
        grid_spec=pltpu.PrefetchScalarGridSpec(
            num_scalar_prefetch=2, grid=(heads,), in_specs=in_specs, out_specs=out_specs
        ),
        out_shape=out_shape,
        compiler_params=pltpu.CompilerParams(vmem_limit_bytes=VMEM),
        cost_estimate=pl.CostEstimate(
            flops=8 * rows * heads * HEAD * span * len(kvs),
            bytes_accessed=4 * rows * width,
            transcendentals=rows * heads * span * len(kvs),
        ),
    )(meta, lens, *args)


def combine_kernel(group, meta, pieces, out):
    yl = meta[4]

    def one(t, _):
        spot = t // NL * NL + lax.rem(t + yl, NL)
        for at in range(0, pieces.shape[2], HEAD):
            values, weights = [], []
            for half in range(NY):
                tail = pieces[half * NX * NL + t, group:, at : at + HEAD].astype(F32)
                line = tail[0:1, :] + tail[1:2, :] + tail[2:3, :]
                wide = jnp.broadcast_to(line, (HEAD, HEAD)).T
                weights.append(jnp.where(yl == 0, wide[:group, :], wide[group : 2 * group, :]))
                values.append(pieces[half * NX * NL + t, 0:group, at : at + HEAD].astype(F32))
            top = jnp.maximum(weights[0], weights[1])
            a, b = jnp.exp2(weights[0] - top), jnp.exp2(weights[1] - top)
            joined = (values[0] * a + values[1] * b) / (a + b)
            out[:, pl.ds(pl.multiple_of(spot * pieces.shape[2] + at, HEAD), HEAD)] = joined.astype(BF16)
        return 0

    lax.fori_loop(0, NX * NL, one, 0, unroll=True)


def combine(meta, pieces):
    group, width = pieces.shape[1] - TAIL, pieces.shape[2]
    return pl.pallas_call(
        functools.partial(combine_kernel, group),
        in_specs=[pl.BlockSpec(memory_space=pltpu.SMEM), pl.BlockSpec(memory_space=pltpu.VMEM)],
        out_specs=pl.BlockSpec(memory_space=pltpu.VMEM),
        out_shape=jax.ShapeDtypeStruct((group, NX * NL * width), BF16),
        compiler_params=pltpu.CompilerParams(vmem_limit_bytes=VMEM),
    )(meta, pieces)


def project_kernel(*refs):
    blocks, weight, (keep, send) = refs[:-3], refs[-3], refs[-2:]
    total = jnp.dot(
        jnp.concatenate([block[...] for block in blocks], 0), weight[...], preferred_element_type=F32
    )

    @pl.when(pl.program_id(0) < 2)
    def _():
        keep[...] = total

    @pl.when(pl.program_id(0) >= 2)
    def _():
        send[...] = total.astype(BF16)


def project(blocks, weight):
    rows = blocks[0].shape[0] * len(blocks)
    depth, width = weight.shape
    tile = width // 4
    place = lambda j: 2 * (j % 2) + j // 2
    whole = pl.BlockSpec(blocks[0].shape, lambda j: (0, 0))
    return pl.pallas_call(
        project_kernel,
        grid=(4,),
        in_specs=[whole] * len(blocks) + [pl.BlockSpec((depth, tile), lambda j: (0, place(j)))],
        out_specs=[
            pl.BlockSpec((rows, tile), lambda j: (0, jnp.minimum(j, 1))),
            pl.BlockSpec((rows, tile), lambda j: (0, jnp.maximum(j - 2, 0))),
        ],
        out_shape=[
            jax.ShapeDtypeStruct((rows, width // 2), F32),
            jax.ShapeDtypeStruct((rows, width // 2), BF16),
        ],
        compiler_params=pltpu.CompilerParams(vmem_limit_bytes=VMEM),
        cost_estimate=pl.CostEstimate(
            flops=2 * rows * depth * width, bytes_accessed=2 * depth * width, transcendentals=0
        ),
    )(*blocks, weight)


def settle_kernel(order, meta, *refs):
    out = refs[-1]
    width = out.shape[3]
    z, yh = meta[0], meta[1]
    for part, shifts in enumerate(order):
        kept, near = refs[2 * part : 2 * part + 2]
        group = kept.shape[0] // len(shifts)
        for at, shift in enumerate(shifts):
            zs = lax.rem(z + shift + NZ, NZ)
            here = pl.ds(at * group, group)
            total = (kept[here, :] + near[here, :].astype(F32)).astype(BF16)
            for half in range(NY):
                out[lax.rem(yh + half, NY), zs] = total[:, half * width : (half + 1) * width]


def settle(meta, order, parts):
    rows = sum(part[0].shape[0] for part in parts)
    width = parts[0][0].shape[1] // NY
    flat = [array for part in parts for array in part]
    return pl.pallas_call(
        functools.partial(settle_kernel, order),
        in_specs=[pl.BlockSpec(memory_space=pltpu.SMEM)] + [pl.BlockSpec(memory_space=pltpu.VMEM)] * len(flat),
        out_specs=pl.BlockSpec(memory_space=pltpu.VMEM),
        out_shape=jax.ShapeDtypeStruct((NY, NZ, rows // NZ, width), BF16),
        compiler_params=pltpu.CompilerParams(vmem_limit_bytes=VMEM),
    )(meta, *flat)


def shards(queries, stored_keys, stored_values, fresh_keys, fresh_values, cache_lengths, out_weight):
    cache, fresh = stored_keys.shape[0], fresh_keys.shape[0]
    z, yh, core, x, yl = [lax.axis_index(name) for name in AXES]
    meta = jnp.stack([z, yh, core, x, yl]).astype(jnp.int32)

    kv = jnp.concatenate(
        [
            jnp.concatenate([stored_keys, stored_values], 1),
            jnp.concatenate([fresh_keys, fresh_values], 1),
        ],
        0,
    )
    forth, back = shift_z(kv, 1), shift_z(kv, -1)
    twin_kv = swap(kv, b=1)

    half = queries.shape[1] // 2
    mine = lax.dynamic_slice_in_dim(queries, core * half, half, 1)
    theirs = lax.dynamic_slice_in_dim(queries, (1 - core) * half, half, 1)
    received = swap(theirs, b=1)
    near = jnp.where(
        core == 0,
        jnp.concatenate([mine, received], 0),
        jnp.concatenate([received, mine], 0),
    )
    far = swap(near, a=1)
    q = jnp.where(yh == 0, jnp.concatenate([near, far], 0), jnp.concatenate([far, near], 0))

    blocks = [(kv, 0, 0, 0), (twin_kv, 0, 0, 1)]
    state = None
    for step in range(1, 5):
        last = step == 4
        if step > 1:
            forth, back, state = lax.optimization_barrier((forth, back, state))
        theirs = swap(forth if last else jnp.concatenate([forth, back], 0), b=1)
        blocks += [(forth, 0, -step, 0)] + ([] if last else [(back, 0, step, 0)])
        later = [(theirs, 0, -step, 1)] + ([] if last else [(theirs, 1, step, 1)])
        if last:
            blocks += later
        else:
            ahead, behind = shift_z(forth, 1), shift_z(back, -1) if step < 3 else None
        state = attend(meta, cache_lengths, q, blocks, state, last, cache, fresh)
        if not last:
            forth, back, blocks = ahead, behind, later
    pieces = state

    depth = out_weight.shape[0] // 4
    weight, _ = lax.optimization_barrier((out_weight, received))
    block = lambda value, at, rows: lax.dynamic_slice_in_dim(value, at * rows, rows, 0)
    wide = jnp.concatenate(
        [block(weight, core, 2 * depth), swap(block(weight, 1 - core, 2 * depth), b=1)], 1
    )
    keep, give = block(wide, yh, depth), block(wide, 1 - yh, depth)
    wide = jnp.concatenate(
        [
            jnp.concatenate([keep, swap(give, a=1)], 1),
            jnp.concatenate([swap(keep, d=1), swap(give, a=1, d=1)], 1),
        ],
        0,
    )
    weight = lax.all_gather(wide, "x", axis=0, tiled=True)

    group, width = pieces.shape[2], pieces.shape[3]
    pieces = lax.all_to_all(
        pieces.reshape(NY * NZ, group, width), ("yh", "x", "yl"), split_axis=0, concat_axis=0, tiled=True
    )
    a = combine(meta, pieces)
    forth, back = [a], [a]
    for _ in range(3):
        forth.append(shift_z(forth[-1], 1))
        back.append(shift_z(back[-1], -1))
    forth.append(shift_z(forth[-1], 1))

    def share(blocks):
        kept, sent = project(blocks, weight)
        return kept, swap(sent, b=1)

    order = ((0, -1, 1, -2, 2), (-3, 3, -4))
    first = share([a, forth[1], back[1], forth[2], back[2]])
    second = share([forth[3], back[3], forth[4]])
    settled = settle(meta, order, (first, second))
    rows, width = settled.shape[2:]
    home = lax.all_to_all(
        settled.reshape(NY * NZ, rows, width), ("yh", "x", "yl"), split_axis=0, concat_axis=0, tiled=True
    ).reshape(NY, NZ * rows, width)
    return (home[0].astype(F32) + home[1].astype(F32)).astype(BF16)


def solution(mesh):
    split = Mesh(mesh.devices.reshape(NZ, NY, NC, NX, NL), AXES)
    ctx, tp = ("z", "yh", "core"), ("x", "yl")
    spec = P(ctx, tp)
    return jax.shard_map(
        shards,
        mesh=split,
        in_specs=(spec, spec, spec, spec, spec, P(), P(tp, ctx)),
        out_specs=P(tp, ctx),
        check_vma=False,
    )
```

```python
import functools
import math

import jax
import jax.numpy as jnp
from jax import lax
from jax.experimental import pallas as pl
from jax.experimental.pallas import tpu as pltpu
from jax.sharding import Mesh
from jax.sharding import PartitionSpec as P

HEAD = 128
NZ, NY, NC, NX, NL = 8, 2, 2, 4, 2
NEG = -1e30
VMEM = 16 * 1024 * 1024
AXES = ("z", "yh", "core", "x", "yl")
TILE = 256
TAIL = 16
F32 = jnp.float32
BF16 = jnp.bfloat16


def permute(value, move):
    pairs = []
    for z in range(NZ):
        for yh in range(NY):
            for c in range(NC):
                for x in range(NX):
                    for yl in range(NL):
                        z2, yh2, c2, x2, yl2 = move(z, yh, c, x, yl)
                        source = ((z * NY + yh) * NC + c) * NX * NL + x * NL + yl
                        target = (((z2 % NZ) * NY + yh2) * NC + c2) * NX * NL + (x2 % NX) * NL + yl2
                        pairs.append((source, target))
    return lax.ppermute(value, AXES, pairs)


def meet_up(value):
    return permute(value, lambda z, yh, c, x, yl: (z + 1 - 2 * (z % 2), yh, c, x, yl))


def meet_down(value):
    return permute(value, lambda z, yh, c, x, yl: (z - 1 + 2 * (z % 2), yh, c, x, yl))


def shifted(z, shift):
    return lax.rem(z + shift * (1 - 2 * lax.rem(z, 2)) + NZ, NZ)


def swap(value, a=0, b=0, d=0):
    return permute(value, lambda z, yh, c, x, yl: (z, yh ^ a, c ^ b, x, yl ^ d))


def attend_kernel(sources, heads, which, last, cache, fresh, meta, lens, q_ref, *refs):
    count = len(sources)
    kv_refs, refs = refs[:count], refs[count:]
    rows = q_ref.shape[0]
    group = rows // (NX * NL)
    z, yh, core = meta[0], meta[1], meta[2]
    factor = math.log2(math.e) / math.sqrt(HEAD)

    def head(h, base, before):
        first = before is None
        lanes = pl.ds(pl.multiple_of(h * HEAD, HEAD), HEAD)
        q_lanes = pl.ds(pl.multiple_of((base + h) * HEAD, HEAD), HEAD)

        def score(start):
            q = q_ref[start : start + TILE, q_lanes]
            parts, top = [], None
            for kv, (at, shift, other) in zip(kv_refs, sources):
                span = slice(at * (cache + fresh), (at + 1) * (cache + fresh))
                zs = shifted(z, shift)
                mine = yh * NC + (1 - core if other else core)
                s = lax.dot_general(
                    q, kv[span, :HEAD], (((1,), (1,)), ((), ())), preferred_element_type=F32
                )
                col = lax.broadcasted_iota(jnp.int32, (1, cache), 1)
                stored = s[:, :cache] + jnp.where(col < lens[zs * NY * NC + mine], 0.0, NEG)
                if shift == 0:
                    row = start + lax.broadcasted_iota(jnp.int32, (TILE, fresh), 0)
                    col = mine * fresh + lax.broadcasted_iota(jnp.int32, (TILE, fresh), 1)
                    new = jnp.where(col <= row, s[:, cache:], NEG)
                else:
                    new = s[:, cache:] + jnp.where(zs < z, 0.0, NEG)
                s = jnp.concatenate([stored, new], 1)
                parts.append(s)
                for lane in range(0, cache + fresh, HEAD):
                    piece = s[:, lane : lane + HEAD]
                    top = piece if top is None else jnp.maximum(top, piece)
            return parts, top

        def absorb(start, parts, top):
            here = slice(start, start + TILE)
            m = top.max(axis=1, keepdims=True)
            if first:
                l, acc = None, None
            else:
                acc_in, top_in, sum_in = before
                old = top_in[here, lanes]
                m = jnp.maximum(m, old)
                alpha = jnp.exp2((old - m) * factor)
                m = m[:, 0:1]
                l = sum_in[here, lanes] * alpha
                acc = acc_in[here, lanes] * alpha
            for kv, (at, _, _), s in zip(kv_refs, sources, parts):
                span = slice(at * (cache + fresh), (at + 1) * (cache + fresh))
                p = jnp.exp2((s - m) * factor)
                for lane in range(0, cache + fresh, HEAD):
                    piece = p[:, lane : lane + HEAD]
                    l = piece if l is None else l + piece
                term = jnp.dot(p.astype(BF16), kv[span, HEAD:], preferred_element_type=F32)
                acc = term if acc is None else acc + term
            if not last:
                acc_out, top_out, sum_out = refs[:3]
                acc_out[here, lanes] = acc
                top_out[here, lanes] = jnp.broadcast_to(m, (TILE, HEAD))
                sum_out[here, lanes] = l
                return
            out_ref = refs[-1]
            half = base // heads
            l = l.sum(axis=1, keepdims=True)
            out = (acc / l).astype(BF16)
            lse = m * factor + jnp.log2(l)
            for at in range(0, TILE, group):
                out_ref[half, (start + at) // group, 0:group, lanes] = out[at : at + group, :]
            for at in range(0, TILE, 2 * group):
                line = jnp.broadcast_to(lse[at : at + 2 * group, :], (2 * group, HEAD)).T[0:1, :]
                high = line.astype(BF16).astype(F32)
                middle = (line - high).astype(BF16).astype(F32)
                low = line - high - middle
                kind = lax.broadcasted_iota(jnp.int32, (TAIL, HEAD), 0)
                tail = jnp.where(kind == 0, high, jnp.where(kind == 1, middle, low)).astype(BF16)
                for odd in range(2):
                    out_ref[half, (start + at) // group + odd, group : group + TAIL, lanes] = tail

        starts = list(range(0, rows, TILE))
        now = score(starts[0])
        for at, start in enumerate(starts):
            later = score(starts[at + 1]) if at + 1 < len(starts) else None
            absorb(start, *now)
            now = later
        return 0

    if last:
        for half in range(NY):
            lax.fori_loop(0, heads, lambda h, _: head(h, half * heads, refs[3 * half : 3 * half + 3]), 0)
    else:
        lax.fori_loop(0, heads, lambda h, _: head(h, which * heads, None), 0)


def attend(meta, lens, q, kvs, which, state, cache, fresh):
    rows, width = q.shape
    last = state is not None
    heads = width // HEAD // NY
    span = cache + fresh
    args = [meta, lens, q] + [entry[0] for entry in kvs]
    if last:
        args += [array for half in state for array in half]
        group = rows // (NX * NL)
        out_shape = jax.ShapeDtypeStruct((NY, NX * NL, group + TAIL, heads * HEAD), BF16)
    else:
        out_shape = [jax.ShapeDtypeStruct((rows, heads * HEAD), F32)] * 3
    whole = pl.BlockSpec(memory_space=pltpu.VMEM)
    scalar = pl.BlockSpec(memory_space=pltpu.SMEM)
    out = pl.pallas_call(
        functools.partial(
            attend_kernel, tuple(entry[1:] for entry in kvs), heads, which, last, cache, fresh
        ),
        in_specs=[scalar, scalar] + [whole] * (len(args) - 2),
        out_specs=whole if last else [whole] * 3,
        out_shape=out_shape,
        compiler_params=pltpu.CompilerParams(vmem_limit_bytes=VMEM),
        cost_estimate=pl.CostEstimate(
            flops=4 * rows * heads * HEAD * span * len(kvs) * (2 if last else 1),
            bytes_accessed=4 * rows * width,
            transcendentals=rows * heads * span * len(kvs),
        ),
    )(*args)
    return out if last else tuple(out)


def combine_kernel(group, meta, pieces, out):
    yl = meta[4]

    def one(t, _):
        spot = t // NL * NL + lax.rem(t + yl, NL)
        for at in range(0, pieces.shape[2], HEAD):
            values, weights = [], []
            for half in range(NY):
                tail = pieces[half * NX * NL + t, group:, at : at + HEAD].astype(F32)
                line = tail[0:1, :] + tail[1:2, :] + tail[2:3, :]
                wide = jnp.broadcast_to(line, (HEAD, HEAD)).T
                weights.append(jnp.where(yl == 0, wide[:group, :], wide[group : 2 * group, :]))
                values.append(pieces[half * NX * NL + t, 0:group, at : at + HEAD].astype(F32))
            top = jnp.maximum(weights[0], weights[1])
            a, b = jnp.exp2(weights[0] - top), jnp.exp2(weights[1] - top)
            joined = (values[0] * a + values[1] * b) / (a + b)
            out[:, pl.ds(pl.multiple_of(spot * pieces.shape[2] + at, HEAD), HEAD)] = joined.astype(BF16)
        return 0

    lax.fori_loop(0, NX * NL, one, 0, unroll=True)


def combine(meta, pieces):
    group, width = pieces.shape[1] - TAIL, pieces.shape[2]
    return pl.pallas_call(
        functools.partial(combine_kernel, group),
        in_specs=[pl.BlockSpec(memory_space=pltpu.SMEM), pl.BlockSpec(memory_space=pltpu.VMEM)],
        out_specs=pl.BlockSpec(memory_space=pltpu.VMEM),
        out_shape=jax.ShapeDtypeStruct((group, NX * NL * width), BF16),
        compiler_params=pltpu.CompilerParams(vmem_limit_bytes=VMEM),
    )(meta, pieces)


def project_kernel(*refs):
    blocks, weight, (keep, send) = refs[:-3], refs[-3], refs[-2:]
    total = jnp.dot(
        jnp.concatenate([block[...] for block in blocks], 0), weight[...], preferred_element_type=F32
    )

    @pl.when(pl.program_id(0) < 2)
    def _():
        keep[...] = total

    @pl.when(pl.program_id(0) >= 2)
    def _():
        send[...] = total.astype(BF16)


def project(blocks, weight):
    rows = blocks[0].shape[0] * len(blocks)
    depth, width = weight.shape
    tile = width // 4
    place = lambda j: 2 * (j % 2) + j // 2
    whole = pl.BlockSpec(blocks[0].shape, lambda j: (0, 0))
    return pl.pallas_call(
        project_kernel,
        grid=(4,),
        in_specs=[whole] * len(blocks) + [pl.BlockSpec((depth, tile), lambda j: (0, place(j)))],
        out_specs=[
            pl.BlockSpec((rows, tile), lambda j: (0, jnp.minimum(j, 1))),
            pl.BlockSpec((rows, tile), lambda j: (0, jnp.maximum(j - 2, 0))),
        ],
        out_shape=[
            jax.ShapeDtypeStruct((rows, width // 2), F32),
            jax.ShapeDtypeStruct((rows, width // 2), BF16),
        ],
        compiler_params=pltpu.CompilerParams(vmem_limit_bytes=VMEM),
        cost_estimate=pl.CostEstimate(
            flops=2 * rows * depth * width, bytes_accessed=2 * depth * width, transcendentals=0
        ),
    )(*blocks, weight)


def settle_kernel(order, meta, *refs):
    out = refs[-1]
    width = out.shape[3]
    z, yh = meta[0], meta[1]
    for part, shifts in enumerate(order):
        kept, near = refs[2 * part : 2 * part + 2]
        group = kept.shape[0] // len(shifts)
        for at, shift in enumerate(shifts):
            zs = shifted(z, shift)
            here = pl.ds(at * group, group)
            total = (kept[here, :] + near[here, :].astype(F32)).astype(BF16)
            for half in range(NY):
                out[lax.rem(yh + half, NY), zs] = total[:, half * width : (half + 1) * width]


def settle(meta, order, parts):
    rows = sum(part[0].shape[0] for part in parts)
    width = parts[0][0].shape[1] // NY
    flat = [array for part in parts for array in part]
    return pl.pallas_call(
        functools.partial(settle_kernel, order),
        in_specs=[pl.BlockSpec(memory_space=pltpu.SMEM)] + [pl.BlockSpec(memory_space=pltpu.VMEM)] * len(flat),
        out_specs=pl.BlockSpec(memory_space=pltpu.VMEM),
        out_shape=jax.ShapeDtypeStruct((NY, NZ, rows // NZ, width), BF16),
        compiler_params=pltpu.CompilerParams(vmem_limit_bytes=VMEM),
    )(meta, *flat)


def shards(queries, stored_keys, stored_values, fresh_keys, fresh_values, cache_lengths, out_weight):
    cache, fresh = stored_keys.shape[0], fresh_keys.shape[0]
    z, yh, core, x, yl = [lax.axis_index(name) for name in AXES]
    meta = jnp.stack([z, yh, core, x, yl]).astype(jnp.int32)

    kv = jnp.concatenate(
        [
            jnp.concatenate([stored_keys, stored_values], 1),
            jnp.concatenate([fresh_keys, fresh_values], 1),
        ],
        0,
    )
    ahead, behind = meet_up(kv), meet_down(kv)
    twin_kv = swap(kv, b=1)

    depth = out_weight.shape[0] // 4
    block = lambda value, at, rows: lax.dynamic_slice_in_dim(value, at * rows, rows, 0)
    wide = jnp.concatenate(
        [block(out_weight, core, 2 * depth), swap(block(out_weight, 1 - core, 2 * depth), b=1)], 1
    )
    keep, give = block(wide, yh, depth), block(wide, 1 - yh, depth)
    wide = jnp.concatenate(
        [
            jnp.concatenate([keep, swap(give, a=1)], 1),
            jnp.concatenate([swap(keep, d=1), swap(give, a=1, d=1)], 1),
        ],
        0,
    )

    half = queries.shape[1] // 2
    mine = lax.dynamic_slice_in_dim(queries, core * half, half, 1)
    theirs = swap(lax.dynamic_slice_in_dim(queries, (1 - core) * half, half, 1), b=1)
    near = jnp.concatenate([jnp.where(core == 0, mine, theirs), jnp.where(core == 0, theirs, mine)], 0)
    wide, near, ahead, behind = lax.optimization_barrier((wide, near, ahead, behind))
    weight = lax.all_gather(wide, "x", axis=0, tiled=True)
    far = swap(near, a=1)
    q = jnp.concatenate([jnp.where(yh == 0, near, far), jnp.where(yh == 0, far, near)], 0)

    def both(ahead, behind, step):
        near = [(ahead, 0, step, 0), (behind, 0, -step, 0)]
        return near + [(swap(array, b=1), at, shift, 1) for array, at, shift, _ in near]

    blocks = [(kv, 0, 0, 0), (twin_kv, 0, 0, 1)] + both(ahead, behind, 1)
    ahead, behind = meet_up(behind), meet_down(ahead)
    blocks += both(ahead, behind, 2)
    ahead, behind = meet_up(behind), meet_down(ahead)
    low = attend(meta, cache_lengths, q, blocks, 0, None, cache, fresh)
    ahead, behind, low = lax.optimization_barrier((ahead, behind, low))
    last_blocks = both(ahead, behind, 3)
    ahead = meet_up(behind)
    high = attend(meta, cache_lengths, q, blocks, 1, None, cache, fresh)
    ahead, high = lax.optimization_barrier((ahead, high))
    last_blocks += [(ahead, 0, 4, 0), (swap(ahead, b=1), 0, 4, 1)]
    pieces = attend(meta, cache_lengths, q, last_blocks, None, (low, high), cache, fresh)

    group, width = pieces.shape[2], pieces.shape[3]
    pieces = lax.all_to_all(
        pieces.reshape(NY * NZ, group, width), ("yh", "x", "yl"), split_axis=0, concat_axis=0, tiled=True
    )
    a = combine(meta, pieces)
    ahead, behind = [a], [a]
    for _ in range(3):
        up, down = meet_up(behind[-1]), meet_down(ahead[-1])
        ahead.append(up)
        behind.append(down)
    ahead.append(meet_up(behind[-1]))

    def share(blocks):
        kept, sent = project(blocks, weight)
        return kept, swap(sent, b=1)

    order = ((0, 1, -1, 2, -2), (3, -3, 4))
    first = share([a, ahead[1], behind[1], ahead[2], behind[2]])
    second = share([ahead[3], behind[3], ahead[4]])
    settled = settle(meta, order, (first, second))
    rows, width = settled.shape[2:]
    home = lax.all_to_all(
        settled.reshape(NY * NZ, rows, width), ("yh", "x", "yl"), split_axis=0, concat_axis=0, tiled=True
    ).reshape(NY, NZ * rows, width)
    return (home[0].astype(F32) + home[1].astype(F32)).astype(BF16)


def solution(mesh):
    split = Mesh(mesh.devices.reshape(NZ, NY, NC, NX, NL), AXES)
    ctx, tp = ("z", "yh", "core"), ("x", "yl")
    spec = P(ctx, tp)
    return jax.shard_map(
        shards,
        mesh=split,
        in_specs=(spec, spec, spec, spec, spec, P(), P(tp, ctx)),
        out_specs=P(tp, ctx),
        check_vma=False,
    )
```

```python
import functools
import math

import jax
import jax.numpy as jnp
from jax import lax
from jax.experimental import pallas as pl
from jax.experimental.pallas import tpu as pltpu
from jax.sharding import Mesh
from jax.sharding import PartitionSpec as P

HEAD = 128
NZ, NY, NC, NX, NL = 8, 2, 2, 4, 2
NEG = -1e30
VMEM = 16 * 1024 * 1024
AXES = ("z", "yh", "core", "x", "yl")
TILE = 256
TAIL = 16
F32 = jnp.float32
BF16 = jnp.bfloat16


def permute(value, move):
    pairs = []
    for z in range(NZ):
        for yh in range(NY):
            for c in range(NC):
                for x in range(NX):
                    for yl in range(NL):
                        z2, yh2, c2, x2, yl2 = move(z, yh, c, x, yl)
                        source = ((z * NY + yh) * NC + c) * NX * NL + x * NL + yl
                        target = (((z2 % NZ) * NY + yh2) * NC + c2) * NX * NL + (x2 % NX) * NL + yl2
                        pairs.append((source, target))
    return lax.ppermute(value, AXES, pairs)


def meet_up(value):
    return permute(value, lambda z, yh, c, x, yl: (z + 1 - 2 * (z % 2), yh, c, x, yl))


def meet_down(value):
    return permute(value, lambda z, yh, c, x, yl: (z - 1 + 2 * (z % 2), yh, c, x, yl))


def shift_x(value, step):
    return permute(value, lambda z, yh, c, x, yl: (z, yh, c, x + step, yl))


def shifted(z, shift):
    return lax.rem(z + shift * (1 - 2 * lax.rem(z, 2)) + NZ, NZ)


def swap(value, a=0, b=0, d=0):
    return permute(value, lambda z, yh, c, x, yl: (z, yh ^ a, c ^ b, x, yl ^ d))


def attend_kernel(sources, heads, which, last, cache, fresh, meta, lens, q_ref, *refs):
    count = len(sources)
    kv_refs, refs = refs[:count], refs[count:]
    rows = q_ref.shape[0]
    group = rows // (NX * NL)
    z, yh, core = meta[0], meta[1], meta[2]
    factor = math.log2(math.e) / math.sqrt(HEAD)

    def head(h, base, before):
        first = before is None
        lanes = pl.ds(pl.multiple_of(h * HEAD, HEAD), HEAD)
        q_lanes = pl.ds(pl.multiple_of((base + h) * HEAD, HEAD), HEAD)

        def score(start):
            q = q_ref[start : start + TILE, q_lanes]
            parts, top = [], None
            for kv, (at, shift, other) in zip(kv_refs, sources):
                span = slice(at * (cache + fresh), (at + 1) * (cache + fresh))
                zs = shifted(z, shift)
                mine = yh * NC + (1 - core if other else core)
                s = lax.dot_general(
                    q, kv[span, :HEAD], (((1,), (1,)), ((), ())), preferred_element_type=F32
                )
                col = lax.broadcasted_iota(jnp.int32, (1, cache), 1)
                stored = s[:, :cache] + jnp.where(col < lens[zs * NY * NC + mine], 0.0, NEG)
                if shift == 0:
                    row = start + lax.broadcasted_iota(jnp.int32, (TILE, fresh), 0)
                    col = mine * fresh + lax.broadcasted_iota(jnp.int32, (TILE, fresh), 1)
                    new = jnp.where(col <= row, s[:, cache:], NEG)
                else:
                    new = s[:, cache:] + jnp.where(zs < z, 0.0, NEG)
                s = jnp.concatenate([stored, new], 1)
                parts.append(s)
                for lane in range(0, cache + fresh, HEAD):
                    piece = s[:, lane : lane + HEAD]
                    top = piece if top is None else jnp.maximum(top, piece)
            return parts, top

        def absorb(start, parts, top):
            here = slice(start, start + TILE)
            m = top.max(axis=1, keepdims=True)
            if first:
                l, acc = None, None
            else:
                acc_in, top_in, sum_in = before
                old = top_in[here, lanes]
                m = jnp.maximum(m, old)
                alpha = jnp.exp2((old - m) * factor)
                m = m[:, 0:1]
                l = sum_in[here, lanes] * alpha
                acc = acc_in[here, lanes] * alpha
            for kv, (at, _, _), s in zip(kv_refs, sources, parts):
                span = slice(at * (cache + fresh), (at + 1) * (cache + fresh))
                p = jnp.exp2((s - m) * factor)
                for lane in range(0, cache + fresh, HEAD):
                    piece = p[:, lane : lane + HEAD]
                    l = piece if l is None else l + piece
                term = jnp.dot(p.astype(BF16), kv[span, HEAD:], preferred_element_type=F32)
                acc = term if acc is None else acc + term
            if not last:
                acc_out, top_out, sum_out = refs[:3]
                acc_out[here, lanes] = acc
                top_out[here, lanes] = jnp.broadcast_to(m, (TILE, HEAD))
                sum_out[here, lanes] = l
                return
            out_ref = refs[-1]
            half = base // heads
            l = l.sum(axis=1, keepdims=True)
            out = (acc / l).astype(BF16)
            lse = m * factor + jnp.log2(l)
            for at in range(0, TILE, group):
                out_ref[half, (start + at) // group, 0:group, lanes] = out[at : at + group, :]
            for at in range(0, TILE, 2 * group):
                line = jnp.broadcast_to(lse[at : at + 2 * group, :], (2 * group, HEAD)).T[0:1, :]
                high = line.astype(BF16).astype(F32)
                middle = (line - high).astype(BF16).astype(F32)
                low = line - high - middle
                kind = lax.broadcasted_iota(jnp.int32, (TAIL, HEAD), 0)
                tail = jnp.where(kind == 0, high, jnp.where(kind == 1, middle, low)).astype(BF16)
                for odd in range(2):
                    out_ref[half, (start + at) // group + odd, group : group + TAIL, lanes] = tail

        starts = list(range(0, rows, TILE))
        now = score(starts[0])
        for at, start in enumerate(starts):
            later = score(starts[at + 1]) if at + 1 < len(starts) else None
            absorb(start, *now)
            now = later
        return 0

    if last:
        for half in range(NY):
            lax.fori_loop(0, heads, lambda h, _: head(h, half * heads, refs[3 * half : 3 * half + 3]), 0)
    else:
        lax.fori_loop(0, heads, lambda h, _: head(h, which * heads, None), 0)


def attend(meta, lens, q, kvs, which, state, cache, fresh):
    rows, width = q.shape
    last = state is not None
    heads = width // HEAD // NY
    span = cache + fresh
    args = [meta, lens, q] + [entry[0] for entry in kvs]
    if last:
        args += [array for half in state for array in half]
        group = rows // (NX * NL)
        out_shape = jax.ShapeDtypeStruct((NY, NX * NL, group + TAIL, heads * HEAD), BF16)
    else:
        out_shape = [jax.ShapeDtypeStruct((rows, heads * HEAD), F32)] * 3
    whole = pl.BlockSpec(memory_space=pltpu.VMEM)
    scalar = pl.BlockSpec(memory_space=pltpu.SMEM)
    out = pl.pallas_call(
        functools.partial(
            attend_kernel, tuple(entry[1:] for entry in kvs), heads, which, last, cache, fresh
        ),
        in_specs=[scalar, scalar] + [whole] * (len(args) - 2),
        out_specs=whole if last else [whole] * 3,
        out_shape=out_shape,
        compiler_params=pltpu.CompilerParams(vmem_limit_bytes=VMEM),
        cost_estimate=pl.CostEstimate(
            flops=4 * rows * heads * HEAD * span * len(kvs) * (2 if last else 1),
            bytes_accessed=4 * rows * width,
            transcendentals=rows * heads * span * len(kvs),
        ),
    )(*args)
    return out if last else tuple(out)


def combine_kernel(group, meta, pieces, out):
    x, yl = meta[3], meta[4]

    def one(t, _):
        spot = lax.rem(t // NL - x + NX, NX) * NL + lax.rem(t + yl, NL)
        for at in range(0, pieces.shape[2], HEAD):
            values, weights = [], []
            for half in range(NY):
                tail = pieces[half * NX * NL + t, group:, at : at + HEAD].astype(F32)
                line = tail[0:1, :] + tail[1:2, :] + tail[2:3, :]
                wide = jnp.broadcast_to(line, (HEAD, HEAD)).T
                weights.append(jnp.where(yl == 0, wide[:group, :], wide[group : 2 * group, :]))
                values.append(pieces[half * NX * NL + t, 0:group, at : at + HEAD].astype(F32))
            top = jnp.maximum(weights[0], weights[1])
            a, b = jnp.exp2(weights[0] - top), jnp.exp2(weights[1] - top)
            joined = (values[0] * a + values[1] * b) / (a + b)
            out[:, pl.ds(pl.multiple_of(spot * pieces.shape[2] + at, HEAD), HEAD)] = joined.astype(BF16)
        return 0

    lax.fori_loop(0, NX * NL, one, 0, unroll=True)


def combine(meta, pieces):
    group, width = pieces.shape[1] - TAIL, pieces.shape[2]
    return pl.pallas_call(
        functools.partial(combine_kernel, group),
        in_specs=[pl.BlockSpec(memory_space=pltpu.SMEM), pl.BlockSpec(memory_space=pltpu.VMEM)],
        out_specs=pl.BlockSpec(memory_space=pltpu.VMEM),
        out_shape=jax.ShapeDtypeStruct((group, NX * NL * width), BF16),
        compiler_params=pltpu.CompilerParams(vmem_limit_bytes=VMEM),
    )(meta, pieces)


def project_kernel(count, *refs):
    blocks, weights, (keep, send) = refs[:count], refs[count:-2], refs[-2:]
    total, at = None, 0
    for weight in weights:
        depth = weight.shape[0]
        a = jnp.concatenate([block[:, at : at + depth] for block in blocks], 0)
        term = jnp.dot(a, weight[...], preferred_element_type=F32)
        total = term if total is None else total + term
        at += depth

    @pl.when(pl.program_id(0) < NY)
    def _():
        keep[...] = total

    @pl.when(pl.program_id(0) >= NY)
    def _():
        send[...] = total.astype(BF16)


def project(blocks, weights):
    rows = blocks[0].shape[0] * len(blocks)
    width = weights[0].shape[1]
    tile = width // (NY * NC)
    place = lambda j: j % NY * NC + j // NY
    whole = pl.BlockSpec(blocks[0].shape, lambda j: (0, 0))
    return pl.pallas_call(
        functools.partial(project_kernel, len(blocks)),
        grid=(NC * NY,),
        in_specs=[whole] * len(blocks)
        + [pl.BlockSpec((weight.shape[0], tile), lambda j: (0, place(j))) for weight in weights],
        out_specs=[
            pl.BlockSpec((rows, tile), lambda j: (0, jnp.minimum(j, NY - 1))),
            pl.BlockSpec((rows, tile), lambda j: (0, jnp.maximum(j - NY, 0))),
        ],
        out_shape=[
            jax.ShapeDtypeStruct((rows, NY * tile), F32),
            jax.ShapeDtypeStruct((rows, NY * tile), BF16),
        ],
        compiler_params=pltpu.CompilerParams(vmem_limit_bytes=VMEM),
        cost_estimate=pl.CostEstimate(
            flops=2 * rows * blocks[0].shape[1] * width,
            bytes_accessed=2 * blocks[0].shape[1] * width,
            transcendentals=0,
        ),
    )(*blocks, *weights)


def settle_kernel(order, meta, *refs):
    out = refs[-1]
    width = out.shape[3]
    z, yh = meta[0], meta[1]
    for part, shifts in enumerate(order):
        kept, near = refs[2 * part : 2 * part + 2]
        group = kept.shape[0] // len(shifts)
        for at, shift in enumerate(shifts):
            zs = shifted(z, shift)
            here = pl.ds(at * group, group)
            total = (kept[here, :] + near[here, :].astype(F32)).astype(BF16)
            for half in range(NY):
                out[lax.rem(yh + half, NY), zs] = total[:, half * width : (half + 1) * width]


def settle(meta, order, parts):
    rows = sum(part[0].shape[0] for part in parts)
    width = parts[0][0].shape[1] // NY
    flat = [array for part in parts for array in part]
    return pl.pallas_call(
        functools.partial(settle_kernel, order),
        in_specs=[pl.BlockSpec(memory_space=pltpu.SMEM)] + [pl.BlockSpec(memory_space=pltpu.VMEM)] * len(flat),
        out_specs=pl.BlockSpec(memory_space=pltpu.VMEM),
        out_shape=jax.ShapeDtypeStruct((NY, NZ, rows // NZ, width), BF16),
        compiler_params=pltpu.CompilerParams(vmem_limit_bytes=VMEM),
    )(meta, *flat)


def shards(queries, stored_keys, stored_values, fresh_keys, fresh_values, cache_lengths, out_weight):
    cache, fresh = stored_keys.shape[0], fresh_keys.shape[0]
    z, yh, core, x, yl = [lax.axis_index(name) for name in AXES]
    meta = jnp.stack([z, yh, core, x, yl]).astype(jnp.int32)

    kv = jnp.concatenate(
        [
            jnp.concatenate([stored_keys, stored_values], 1),
            jnp.concatenate([fresh_keys, fresh_values], 1),
        ],
        0,
    )
    ahead, behind = meet_up(kv), meet_down(kv)
    twin_kv = swap(kv, b=1)

    half = queries.shape[1] // 2
    mine = lax.dynamic_slice_in_dim(queries, core * half, half, 1)
    theirs = swap(lax.dynamic_slice_in_dim(queries, (1 - core) * half, half, 1), b=1)
    near = jnp.concatenate([jnp.where(core == 0, mine, theirs), jnp.where(core == 0, theirs, mine)], 0)
    far = swap(near, a=1)
    q = jnp.concatenate([jnp.where(yh == 0, near, far), jnp.where(yh == 0, far, near)], 0)

    ahead, behind, out_weight = lax.optimization_barrier((ahead, behind, out_weight))
    depth = out_weight.shape[0] // 4
    block = lambda value, at, rows: lax.dynamic_slice_in_dim(value, at * rows, rows, 0)
    wide = jnp.concatenate(
        [block(out_weight, core, 2 * depth), swap(block(out_weight, 1 - core, 2 * depth), b=1)], 1
    )
    keep, give = block(wide, yh, depth), block(wide, 1 - yh, depth)
    quarters = [keep, swap(give, a=1), swap(keep, d=1), swap(give, a=1, d=1)]

    def both(ahead, behind, step):
        near = [(ahead, 0, step, 0), (behind, 0, -step, 0)]
        return near + [(swap(array, b=1), at, shift, 1) for array, at, shift, _ in near]

    blocks = [(kv, 0, 0, 0), (twin_kv, 0, 0, 1)] + both(ahead, behind, 1)
    ahead, behind = meet_up(behind), meet_down(ahead)
    blocks += both(ahead, behind, 2)
    ahead, behind = meet_up(behind), meet_down(ahead)
    low = attend(meta, cache_lengths, q, blocks, 0, None, cache, fresh)
    ahead, behind, low, quarters = lax.optimization_barrier((ahead, behind, low, quarters))
    wide = jnp.concatenate(
        [jnp.concatenate(quarters[:2], 1), jnp.concatenate(quarters[2:], 1)], 0
    )
    wide_f, wide_b = shift_x(wide, 1), shift_x(wide, -1)
    last_blocks = both(ahead, behind, 3)
    ahead = meet_up(behind)
    high = attend(meta, cache_lengths, q, blocks, 1, None, cache, fresh)
    ahead, high = lax.optimization_barrier((ahead, high))
    last_blocks += [(ahead, 0, 4, 0), (swap(ahead, b=1), 0, 4, 1)]
    pieces = attend(meta, cache_lengths, q, last_blocks, None, (low, high), cache, fresh)

    group, width = pieces.shape[2], pieces.shape[3]
    pieces = lax.all_to_all(
        pieces.reshape(NY * NZ, group, width), ("yh", "x", "yl"), split_axis=0, concat_axis=0, tiled=True
    )
    a = combine(meta, pieces)
    a, wide_f, wide_b = lax.optimization_barrier((a, wide_f, wide_b))
    weights = [wide, wide_b, shift_x(wide_f[:depth], 1), shift_x(wide_b[depth:], -1), wide_f]
    ahead, behind = [a], [a]
    for _ in range(3):
        up, down = meet_up(behind[-1]), meet_down(ahead[-1])
        ahead.append(up)
        behind.append(down)
    ahead.append(meet_up(behind[-1]))

    def share(blocks):
        kept, sent = project(blocks, weights)
        return kept, swap(sent, b=1)

    order = ((0, 1, -1, 2, -2), (3, -3, 4))
    first = share([a, ahead[1], behind[1], ahead[2], behind[2]])
    second = share([ahead[3], behind[3], ahead[4]])
    settled = settle(meta, order, (first, second))
    rows, width = settled.shape[2:]
    home = lax.all_to_all(
        settled.reshape(NY * NZ, rows, width), ("yh", "x", "yl"), split_axis=0, concat_axis=0, tiled=True
    ).reshape(NY, NZ * rows, width)
    return (home[0].astype(F32) + home[1].astype(F32)).astype(BF16)


def solution(mesh):
    split = Mesh(mesh.devices.reshape(NZ, NY, NC, NX, NL), AXES)
    ctx, tp = ("z", "yh", "core"), ("x", "yl")
    spec = P(ctx, tp)
    return jax.shard_map(
        shards,
        mesh=split,
        in_specs=(spec, spec, spec, spec, spec, P(), P(tp, ctx)),
        out_specs=P(tp, ctx),
        check_vma=False,
    )
```

```python
import functools
import math

import jax
import jax.numpy as jnp
from jax import lax
from jax.experimental import pallas as pl
from jax.experimental.pallas import tpu as pltpu
from jax.sharding import Mesh
from jax.sharding import PartitionSpec as P

HEAD = 128
NZ, NY, NC, NX, NL = 8, 2, 2, 4, 2
NEG = -1e30
VMEM = 16 * 1024 * 1024
AXES = ("z", "yh", "core", "x", "yl")
TILE = 256
TAIL = 16
F32 = jnp.float32
BF16 = jnp.bfloat16


def permute(value, move):
    pairs = []
    for z in range(NZ):
        for yh in range(NY):
            for c in range(NC):
                for x in range(NX):
                    for yl in range(NL):
                        z2, yh2, c2, x2, yl2 = move(z, yh, c, x, yl)
                        source = ((z * NY + yh) * NC + c) * NX * NL + x * NL + yl
                        target = (((z2 % NZ) * NY + yh2) * NC + c2) * NX * NL + (x2 % NX) * NL + yl2
                        pairs.append((source, target))
    return lax.ppermute(value, AXES, pairs)


def meet_up(value):
    return permute(value, lambda z, yh, c, x, yl: (z + 1 - 2 * (z % 2), yh, c, x, yl))


def meet_down(value):
    return permute(value, lambda z, yh, c, x, yl: (z - 1 + 2 * (z % 2), yh, c, x, yl))


def shift_x(value, step):
    return permute(value, lambda z, yh, c, x, yl: (z, yh, c, x + step, yl))


def shifted(z, shift):
    return lax.rem(z + shift * (1 - 2 * lax.rem(z, 2)) + NZ, NZ)


def swap(value, a=0, b=0, d=0):
    return permute(value, lambda z, yh, c, x, yl: (z, yh ^ a, c ^ b, x, yl ^ d))


def attend_kernel(sources, heads, which, last, cache, fresh, meta, lens, q_ref, *refs):
    count = len(sources)
    kv_refs, refs = refs[:count], refs[count:]
    rows = q_ref.shape[0]
    group = rows // (NX * NL)
    z, yh, core = meta[0], meta[1], meta[2]
    factor = math.log2(math.e) / math.sqrt(HEAD)

    def head(h, base, before):
        first = before is None
        lanes = pl.ds(pl.multiple_of(h * HEAD, HEAD), HEAD)
        q_lanes = pl.ds(pl.multiple_of((base + h) * HEAD, HEAD), HEAD)

        def score(start):
            q = q_ref[start : start + TILE, q_lanes]
            parts, top = [], None
            for kv, (at, shift, other) in zip(kv_refs, sources):
                span = slice(at * (cache + fresh), (at + 1) * (cache + fresh))
                zs = shifted(z, shift)
                mine = yh * NC + (1 - core if other else core)
                s = lax.dot_general(
                    q, kv[span, :HEAD], (((1,), (1,)), ((), ())), preferred_element_type=F32
                )
                col = lax.broadcasted_iota(jnp.int32, (1, cache), 1)
                stored = s[:, :cache] + jnp.where(col < lens[zs * NY * NC + mine], 0.0, NEG)
                if shift == 0:
                    row = start + lax.broadcasted_iota(jnp.int32, (TILE, fresh), 0)
                    col = mine * fresh + lax.broadcasted_iota(jnp.int32, (TILE, fresh), 1)
                    new = jnp.where(col <= row, s[:, cache:], NEG)
                else:
                    new = s[:, cache:] + jnp.where(zs < z, 0.0, NEG)
                s = jnp.concatenate([stored, new], 1)
                parts.append(s)
                for lane in range(0, cache + fresh, HEAD):
                    piece = s[:, lane : lane + HEAD]
                    top = piece if top is None else jnp.maximum(top, piece)
            return parts, top

        def absorb(start, parts, top):
            here = slice(start, start + TILE)
            m = top.max(axis=1, keepdims=True)
            if first:
                l, acc = None, None
            else:
                acc_in, top_in, sum_in = before
                old = top_in[here, lanes]
                m = jnp.maximum(m, old)
                alpha = jnp.exp2((old - m) * factor)
                m = m[:, 0:1]
                l = sum_in[here, lanes] * alpha
                acc = acc_in[here, lanes] * alpha
            for kv, (at, _, _), s in zip(kv_refs, sources, parts):
                span = slice(at * (cache + fresh), (at + 1) * (cache + fresh))
                p = jnp.exp2((s - m) * factor)
                for lane in range(0, cache + fresh, HEAD):
                    piece = p[:, lane : lane + HEAD]
                    l = piece if l is None else l + piece
                term = jnp.dot(p.astype(BF16), kv[span, HEAD:], preferred_element_type=F32)
                acc = term if acc is None else acc + term
            if not last:
                acc_out, top_out, sum_out = refs[:3]
                acc_out[here, lanes] = acc
                top_out[here, lanes] = jnp.broadcast_to(m, (TILE, HEAD))
                sum_out[here, lanes] = l
                return
            out_ref = refs[-1]
            half = base // heads
            l = l.sum(axis=1, keepdims=True)
            out = (acc / l).astype(BF16)
            lse = m * factor + jnp.log2(l)
            for at in range(0, TILE, group):
                out_ref[half, (start + at) // group, 0:group, lanes] = out[at : at + group, :]
            for at in range(0, TILE, 2 * group):
                line = jnp.broadcast_to(lse[at : at + 2 * group, :], (2 * group, HEAD)).T[0:1, :]
                high = line.astype(BF16).astype(F32)
                middle = (line - high).astype(BF16).astype(F32)
                low = line - high - middle
                kind = lax.broadcasted_iota(jnp.int32, (TAIL, HEAD), 0)
                tail = jnp.where(kind == 0, high, jnp.where(kind == 1, middle, low)).astype(BF16)
                for odd in range(2):
                    out_ref[half, (start + at) // group + odd, group : group + TAIL, lanes] = tail

        starts = list(range(0, rows, TILE))
        now = score(starts[0])
        for at, start in enumerate(starts):
            later = score(starts[at + 1]) if at + 1 < len(starts) else None
            absorb(start, *now)
            now = later
        return 0

    if last:
        for half in range(NY):
            lax.fori_loop(0, heads, lambda h, _: head(h, half * heads, refs[3 * half : 3 * half + 3]), 0)
    else:
        lax.fori_loop(0, heads, lambda h, _: head(h, which * heads, None), 0)


def attend(meta, lens, q, kvs, which, state, cache, fresh):
    rows, width = q.shape
    last = state is not None
    heads = width // HEAD // NY
    span = cache + fresh
    args = [meta, lens, q] + [entry[0] for entry in kvs]
    if last:
        args += [array for half in state for array in half]
        group = rows // (NX * NL)
        out_shape = jax.ShapeDtypeStruct((NY, NX * NL, group + TAIL, heads * HEAD), BF16)
    else:
        out_shape = [jax.ShapeDtypeStruct((rows, heads * HEAD), F32)] * 3
    whole = pl.BlockSpec(memory_space=pltpu.VMEM)
    scalar = pl.BlockSpec(memory_space=pltpu.SMEM)
    out = pl.pallas_call(
        functools.partial(
            attend_kernel, tuple(entry[1:] for entry in kvs), heads, which, last, cache, fresh
        ),
        in_specs=[scalar, scalar] + [whole] * (len(args) - 2),
        out_specs=whole if last else [whole] * 3,
        out_shape=out_shape,
        compiler_params=pltpu.CompilerParams(vmem_limit_bytes=VMEM),
        cost_estimate=pl.CostEstimate(
            flops=4 * rows * heads * HEAD * span * len(kvs) * (2 if last else 1),
            bytes_accessed=4 * rows * width,
            transcendentals=rows * heads * span * len(kvs),
        ),
    )(*args)
    return out if last else tuple(out)


def combine_kernel(group, meta, pieces, out):
    x, yl = meta[3], meta[4]

    def one(t, _):
        spot = lax.rem(t // NL - x + NX, NX) * NL + lax.rem(t + yl, NL)
        for at in range(0, pieces.shape[2], HEAD):
            values, weights = [], []
            for half in range(NY):
                tail = pieces[half * NX * NL + t, group:, at : at + HEAD].astype(F32)
                line = tail[0:1, :] + tail[1:2, :] + tail[2:3, :]
                wide = jnp.broadcast_to(line, (HEAD, HEAD)).T
                weights.append(jnp.where(yl == 0, wide[:group, :], wide[group : 2 * group, :]))
                values.append(pieces[half * NX * NL + t, 0:group, at : at + HEAD].astype(F32))
            top = jnp.maximum(weights[0], weights[1])
            a, b = jnp.exp2(weights[0] - top), jnp.exp2(weights[1] - top)
            joined = (values[0] * a + values[1] * b) / (a + b)
            out[:, pl.ds(pl.multiple_of(spot * pieces.shape[2] + at, HEAD), HEAD)] = joined.astype(BF16)
        return 0

    lax.fori_loop(0, NX * NL, one, 0, unroll=True)


def combine(meta, pieces):
    group, width = pieces.shape[1] - TAIL, pieces.shape[2]
    return pl.pallas_call(
        functools.partial(combine_kernel, group),
        in_specs=[pl.BlockSpec(memory_space=pltpu.SMEM), pl.BlockSpec(memory_space=pltpu.VMEM)],
        out_specs=pl.BlockSpec(memory_space=pltpu.VMEM),
        out_shape=jax.ShapeDtypeStruct((group, NX * NL * width), BF16),
        compiler_params=pltpu.CompilerParams(vmem_limit_bytes=VMEM),
    )(meta, pieces)


def project_kernel(count, *refs):
    blocks, weights, (keep, send) = refs[:count], refs[count:-2], refs[-2:]
    tile = weights[0].shape[1] // (NY * NC)
    for column in range(NY * NC):
        half, core = column // NC, column % NC
        total, at = None, 0
        for weight in weights:
            depth = weight.shape[0]
            a = jnp.concatenate([block[:, at : at + depth] for block in blocks], 0)
            b = weight[:, column * tile : (column + 1) * tile]
            term = jnp.dot(a, b, preferred_element_type=F32)
            total = term if total is None else total + term
            at += depth
        out = keep if core == 0 else send
        out[:, half * tile : (half + 1) * tile] = total.astype(out.dtype)


def project(blocks, weights):
    rows, depth = blocks[0].shape[0] * len(blocks), blocks[0].shape[1]
    width = weights[0].shape[1]
    whole = pl.BlockSpec(memory_space=pltpu.VMEM)
    return pl.pallas_call(
        functools.partial(project_kernel, len(blocks)),
        in_specs=[whole] * (len(blocks) + len(weights)),
        out_specs=[whole, whole],
        out_shape=[
            jax.ShapeDtypeStruct((rows, width // NC), F32),
            jax.ShapeDtypeStruct((rows, width // NC), BF16),
        ],
        compiler_params=pltpu.CompilerParams(vmem_limit_bytes=VMEM),
        cost_estimate=pl.CostEstimate(
            flops=2 * rows * depth * width, bytes_accessed=2 * depth * width, transcendentals=0
        ),
    )(*blocks, *weights)


def settle_kernel(order, meta, *refs):
    out = refs[-1]
    width = out.shape[3]
    z, yh = meta[0], meta[1]
    for part, shifts in enumerate(order):
        kept, near = refs[2 * part : 2 * part + 2]
        group = kept.shape[0] // len(shifts)
        for at, shift in enumerate(shifts):
            zs = shifted(z, shift)
            here = pl.ds(at * group, group)
            total = (kept[here, :] + near[here, :].astype(F32)).astype(BF16)
            for half in range(NY):
                out[lax.rem(yh + half, NY), zs] = total[:, half * width : (half + 1) * width]


def settle(meta, order, parts):
    rows = sum(part[0].shape[0] for part in parts)
    width = parts[0][0].shape[1] // NY
    flat = [array for part in parts for array in part]
    return pl.pallas_call(
        functools.partial(settle_kernel, order),
        in_specs=[pl.BlockSpec(memory_space=pltpu.SMEM)] + [pl.BlockSpec(memory_space=pltpu.VMEM)] * len(flat),
        out_specs=pl.BlockSpec(memory_space=pltpu.VMEM),
        out_shape=jax.ShapeDtypeStruct((NY, NZ, rows // NZ, width), BF16),
        compiler_params=pltpu.CompilerParams(vmem_limit_bytes=VMEM),
    )(meta, *flat)


def shards(queries, stored_keys, stored_values, fresh_keys, fresh_values, cache_lengths, out_weight):
    cache, fresh = stored_keys.shape[0], fresh_keys.shape[0]
    z, yh, core, x, yl = [lax.axis_index(name) for name in AXES]
    meta = jnp.stack([z, yh, core, x, yl]).astype(jnp.int32)

    kv = jnp.concatenate(
        [
            jnp.concatenate([stored_keys, stored_values], 1),
            jnp.concatenate([fresh_keys, fresh_values], 1),
        ],
        0,
    )
    ahead, behind = meet_up(kv), meet_down(kv)
    twin_kv = swap(kv, b=1)

    half = queries.shape[1] // 2
    mine = lax.dynamic_slice_in_dim(queries, core * half, half, 1)
    theirs = swap(lax.dynamic_slice_in_dim(queries, (1 - core) * half, half, 1), b=1)
    near = jnp.concatenate([jnp.where(core == 0, mine, theirs), jnp.where(core == 0, theirs, mine)], 0)
    far = swap(near, a=1)
    q = jnp.concatenate([jnp.where(yh == 0, near, far), jnp.where(yh == 0, far, near)], 0)

    ahead, behind, out_weight = lax.optimization_barrier((ahead, behind, out_weight))
    depth = out_weight.shape[0] // 4
    block = lambda value, at, rows: lax.dynamic_slice_in_dim(value, at * rows, rows, 0)
    wide = jnp.concatenate(
        [block(out_weight, core, 2 * depth), swap(block(out_weight, 1 - core, 2 * depth), b=1)], 1
    )
    keep, give = block(wide, yh, depth), block(wide, 1 - yh, depth)
    quarters = [keep, swap(give, a=1), swap(keep, d=1), swap(give, a=1, d=1)]

    def both(ahead, behind, step):
        near = [(ahead, 0, step, 0), (behind, 0, -step, 0)]
        return near + [(swap(array, b=1), at, shift, 1) for array, at, shift, _ in near]

    blocks = [(kv, 0, 0, 0), (twin_kv, 0, 0, 1)] + both(ahead, behind, 1)
    ahead, behind = meet_up(behind), meet_down(ahead)
    blocks += both(ahead, behind, 2)
    ahead, behind = meet_up(behind), meet_down(ahead)
    low = attend(meta, cache_lengths, q, blocks, 0, None, cache, fresh)
    ahead, behind, low = lax.optimization_barrier((ahead, behind, low))
    last_blocks = both(ahead, behind, 3)
    ahead = meet_up(behind)
    low, quarters = lax.optimization_barrier((low, quarters))
    wide = jnp.concatenate(
        [jnp.concatenate(quarters[:2], 1), jnp.concatenate(quarters[2:], 1)], 0
    )
    wide_f, wide_b = shift_x(wide, 1), shift_x(wide, -1)
    high = attend(meta, cache_lengths, q, blocks, 1, None, cache, fresh)
    ahead, high = lax.optimization_barrier((ahead, high))
    last_blocks += [(ahead, 0, 4, 0), (swap(ahead, b=1), 0, 4, 1)]
    pieces = attend(meta, cache_lengths, q, last_blocks, None, (low, high), cache, fresh)

    group, width = pieces.shape[2], pieces.shape[3]
    pieces = lax.all_to_all(
        pieces.reshape(NY * NZ, group, width), ("yh", "x", "yl"), split_axis=0, concat_axis=0, tiled=True
    )
    a = combine(meta, pieces)
    a, wide_f, wide_b = lax.optimization_barrier((a, wide_f, wide_b))
    weights = [wide, wide_b, shift_x(wide_f[:depth], 1), shift_x(wide_b[depth:], -1), wide_f]
    ahead, behind = [a], [a]
    for _ in range(3):
        up, down = meet_up(behind[-1]), meet_down(ahead[-1])
        ahead.append(up)
        behind.append(down)
    ahead.append(meet_up(behind[-1]))

    def share(blocks):
        kept, sent = project(blocks, weights)
        return kept, swap(sent, b=1)

    order = ((0, 1, -1, 2, -2), (3, -3, 4))
    first = share([a, ahead[1], behind[1], ahead[2], behind[2]])
    second = share([ahead[3], behind[3], ahead[4]])
    settled = settle(meta, order, (first, second))
    rows, width = settled.shape[2:]
    home = lax.all_to_all(
        settled.reshape(NY * NZ, rows, width), ("yh", "x", "yl"), split_axis=0, concat_axis=0, tiled=True
    ).reshape(NY, NZ * rows, width)
    return (home[0].astype(F32) + home[1].astype(F32)).astype(BF16)


def solution(mesh):
    split = Mesh(mesh.devices.reshape(NZ, NY, NC, NX, NL), AXES)
    ctx, tp = ("z", "yh", "core"), ("x", "yl")
    spec = P(ctx, tp)
    return jax.shard_map(
        shards,
        mesh=split,
        in_specs=(spec, spec, spec, spec, spec, P(), P(tp, ctx)),
        out_specs=P(tp, ctx),
        check_vma=False,
    )
```

```python
import functools
import math

import jax
import jax.numpy as jnp
from jax import lax
from jax.experimental import pallas as pl
from jax.experimental.pallas import tpu as pltpu
from jax.sharding import Mesh
from jax.sharding import PartitionSpec as P

HEAD = 128
NZ, NY, NC, NX, NL = 8, 2, 2, 4, 2
NEG = -1e30
VMEM = 16 * 1024 * 1024
AXES = ("z", "yh", "core", "x", "yl")
TILE = 256
TAIL = 16
F32 = jnp.float32
BF16 = jnp.bfloat16


def permute(value, move):
    pairs = []
    for z in range(NZ):
        for yh in range(NY):
            for c in range(NC):
                for x in range(NX):
                    for yl in range(NL):
                        z2, yh2, c2, x2, yl2 = move(z, yh, c, x, yl)
                        source = ((z * NY + yh) * NC + c) * NX * NL + x * NL + yl
                        target = (((z2 % NZ) * NY + yh2) * NC + c2) * NX * NL + (x2 % NX) * NL + yl2
                        pairs.append((source, target))
    return lax.ppermute(value, AXES, pairs)


def meet_up(value):
    return permute(value, lambda z, yh, c, x, yl: (z + 1 - 2 * (z % 2), yh, c, x, yl))


def meet_down(value):
    return permute(value, lambda z, yh, c, x, yl: (z - 1 + 2 * (z % 2), yh, c, x, yl))


def shift_x(value, step):
    return permute(value, lambda z, yh, c, x, yl: (z, yh, c, x + step, yl))


def shifted(z, shift):
    return lax.rem(z + shift * (1 - 2 * lax.rem(z, 2)) + NZ, NZ)


def swap(value, a=0, b=0, d=0):
    return permute(value, lambda z, yh, c, x, yl: (z, yh ^ a, c ^ b, x, yl ^ d))


def attend_kernel(sources, heads, which, last, cache, fresh, meta, lens, q_ref, *refs):
    count = len(sources)
    kv_refs, refs = refs[:count], refs[count:]
    rows = q_ref.shape[0]
    group = rows // (NX * NL)
    z, yh, core = meta[0], meta[1], meta[2]
    factor = math.log2(math.e) / math.sqrt(HEAD)

    def head(h, base, before):
        first = before is None
        lanes = pl.ds(pl.multiple_of(h * HEAD, HEAD), HEAD)
        q_lanes = pl.ds(pl.multiple_of((base + h) * HEAD, HEAD), HEAD)

        def score(start):
            q = q_ref[start : start + TILE, q_lanes]
            parts, top = [], None
            for kv, (at, shift, other) in zip(kv_refs, sources):
                span = slice(at * (cache + fresh), (at + 1) * (cache + fresh))
                zs = shifted(z, shift)
                mine = yh * NC + (1 - core if other else core)
                s = lax.dot_general(
                    q, kv[span, :HEAD], (((1,), (1,)), ((), ())), preferred_element_type=F32
                )
                col = lax.broadcasted_iota(jnp.int32, (1, cache), 1)
                stored = s[:, :cache] + jnp.where(col < lens[zs * NY * NC + mine], 0.0, NEG)
                if shift == 0:
                    row = start + lax.broadcasted_iota(jnp.int32, (TILE, fresh), 0)
                    col = mine * fresh + lax.broadcasted_iota(jnp.int32, (TILE, fresh), 1)
                    new = jnp.where(col <= row, s[:, cache:], NEG)
                else:
                    new = s[:, cache:] + jnp.where(zs < z, 0.0, NEG)
                s = jnp.concatenate([stored, new], 1)
                parts.append(s)
                for lane in range(0, cache + fresh, HEAD):
                    piece = s[:, lane : lane + HEAD]
                    top = piece if top is None else jnp.maximum(top, piece)
            return parts, top

        def absorb(start, parts, top):
            here = slice(start, start + TILE)
            m = top.max(axis=1, keepdims=True)
            if first:
                l, acc = None, None
            else:
                acc_in, top_in, sum_in = before
                old = top_in[here, lanes]
                m = jnp.maximum(m, old)
                alpha = jnp.exp2((old - m) * factor)
                m = m[:, 0:1]
                l = sum_in[here, lanes] * alpha
                acc = acc_in[here, lanes] * alpha
            for kv, (at, _, _), s in zip(kv_refs, sources, parts):
                span = slice(at * (cache + fresh), (at + 1) * (cache + fresh))
                p = jnp.exp2((s - m) * factor)
                for lane in range(0, cache + fresh, HEAD):
                    piece = p[:, lane : lane + HEAD]
                    l = piece if l is None else l + piece
                term = jnp.dot(p.astype(BF16), kv[span, HEAD:], preferred_element_type=F32)
                acc = term if acc is None else acc + term
            if not last:
                acc_out, top_out, sum_out = refs[:3]
                acc_out[here, lanes] = acc
                top_out[here, lanes] = jnp.broadcast_to(m, (TILE, HEAD))
                sum_out[here, lanes] = l
                return
            out_ref = refs[-1]
            half = base // heads
            l = l.sum(axis=1, keepdims=True)
            out = (acc / l).astype(BF16)
            lse = m * factor + jnp.log2(l)
            for at in range(0, TILE, group):
                out_ref[half, (start + at) // group, 0:group, lanes] = out[at : at + group, :]
            for at in range(0, TILE, 2 * group):
                line = jnp.broadcast_to(lse[at : at + 2 * group, :], (2 * group, HEAD)).T[0:1, :]
                high = line.astype(BF16).astype(F32)
                middle = (line - high).astype(BF16).astype(F32)
                low = line - high - middle
                kind = lax.broadcasted_iota(jnp.int32, (TAIL, HEAD), 0)
                tail = jnp.where(kind == 0, high, jnp.where(kind == 1, middle, low)).astype(BF16)
                for odd in range(2):
                    out_ref[half, (start + at) // group + odd, group : group + TAIL, lanes] = tail

        starts = list(range(0, rows, TILE))
        now = score(starts[0])
        for at, start in enumerate(starts):
            later = score(starts[at + 1]) if at + 1 < len(starts) else None
            absorb(start, *now)
            now = later
        return 0

    if last:
        for half in range(NY):
            lax.fori_loop(0, heads, lambda h, _: head(h, half * heads, refs[3 * half : 3 * half + 3]), 0)
    else:
        lax.fori_loop(0, heads, lambda h, _: head(h, which * heads, None), 0)


def attend(meta, lens, q, kvs, which, state, cache, fresh):
    rows, width = q.shape
    last = state is not None
    heads = width // HEAD // NY
    span = cache + fresh
    args = [meta, lens, q] + [entry[0] for entry in kvs]
    if last:
        args += [array for half in state for array in half]
        group = rows // (NX * NL)
        out_shape = jax.ShapeDtypeStruct((NY, NX * NL, group + TAIL, heads * HEAD), BF16)
    else:
        out_shape = [jax.ShapeDtypeStruct((rows, heads * HEAD), F32)] * 3
    whole = pl.BlockSpec(memory_space=pltpu.VMEM)
    scalar = pl.BlockSpec(memory_space=pltpu.SMEM)
    out = pl.pallas_call(
        functools.partial(
            attend_kernel, tuple(entry[1:] for entry in kvs), heads, which, last, cache, fresh
        ),
        in_specs=[scalar, scalar] + [whole] * (len(args) - 2),
        out_specs=whole if last else [whole] * 3,
        out_shape=out_shape,
        compiler_params=pltpu.CompilerParams(vmem_limit_bytes=VMEM),
        cost_estimate=pl.CostEstimate(
            flops=4 * rows * heads * HEAD * span * len(kvs) * (2 if last else 1),
            bytes_accessed=4 * rows * width,
            transcendentals=rows * heads * span * len(kvs),
        ),
    )(*args)
    return out if last else tuple(out)


def combine_kernel(group, meta, pieces, out):
    x, yl = meta[3], meta[4]

    def one(t, _):
        spot = lax.rem(t // NL - x + NX, NX) * NL + lax.rem(t + yl, NL)
        for at in range(0, pieces.shape[2], HEAD):
            values, weights = [], []
            for half in range(NY):
                tail = pieces[half * NX * NL + t, group:, at : at + HEAD].astype(F32)
                line = tail[0:1, :] + tail[1:2, :] + tail[2:3, :]
                wide = jnp.broadcast_to(line, (HEAD, HEAD)).T
                weights.append(jnp.where(yl == 0, wide[:group, :], wide[group : 2 * group, :]))
                values.append(pieces[half * NX * NL + t, 0:group, at : at + HEAD].astype(F32))
            top = jnp.maximum(weights[0], weights[1])
            a, b = jnp.exp2(weights[0] - top), jnp.exp2(weights[1] - top)
            joined = (values[0] * a + values[1] * b) / (a + b)
            out[:, pl.ds(pl.multiple_of(spot * pieces.shape[2] + at, HEAD), HEAD)] = joined.astype(BF16)
        return 0

    lax.fori_loop(0, NX * NL, one, 0, unroll=True)


def combine(meta, pieces):
    group, width = pieces.shape[1] - TAIL, pieces.shape[2]
    return pl.pallas_call(
        functools.partial(combine_kernel, group),
        in_specs=[pl.BlockSpec(memory_space=pltpu.SMEM), pl.BlockSpec(memory_space=pltpu.VMEM)],
        out_specs=pl.BlockSpec(memory_space=pltpu.VMEM),
        out_shape=jax.ShapeDtypeStruct((group, NX * NL * width), BF16),
        compiler_params=pltpu.CompilerParams(vmem_limit_bytes=VMEM),
    )(meta, pieces)


def project_kernel(count, *refs):
    blocks, weights, (keep, send) = refs[:count], refs[count:-2], refs[-2:]
    tile = weights[0].shape[1] // (NY * NC)
    for column in range(NY * NC):
        half, core = column // NC, column % NC
        total, at = None, 0
        for weight in weights:
            depth = weight.shape[0]
            a = jnp.concatenate([block[:, at : at + depth] for block in blocks], 0)
            b = weight[:, column * tile : (column + 1) * tile]
            term = jnp.dot(a, b, preferred_element_type=F32)
            total = term if total is None else total + term
            at += depth
        out = keep if core == 0 else send
        out[:, half * tile : (half + 1) * tile] = total.astype(out.dtype)


def project(blocks, weights):
    rows, depth = blocks[0].shape[0] * len(blocks), blocks[0].shape[1]
    width = weights[0].shape[1]
    whole = pl.BlockSpec(memory_space=pltpu.VMEM)
    return pl.pallas_call(
        functools.partial(project_kernel, len(blocks)),
        in_specs=[whole] * (len(blocks) + len(weights)),
        out_specs=[whole, whole],
        out_shape=[
            jax.ShapeDtypeStruct((rows, width // NC), F32),
            jax.ShapeDtypeStruct((rows, width // NC), BF16),
        ],
        compiler_params=pltpu.CompilerParams(vmem_limit_bytes=VMEM),
        cost_estimate=pl.CostEstimate(
            flops=2 * rows * depth * width, bytes_accessed=2 * depth * width, transcendentals=0
        ),
    )(*blocks, *weights)


def settle_kernel(order, meta, *refs):
    out = refs[-1]
    width = out.shape[3]
    z, yh = meta[0], meta[1]
    for part, shifts in enumerate(order):
        kept, near = refs[2 * part : 2 * part + 2]
        group = kept.shape[0] // len(shifts)
        for at, shift in enumerate(shifts):
            zs = shifted(z, shift)
            here = pl.ds(at * group, group)
            total = (kept[here, :] + near[here, :].astype(F32)).astype(BF16)
            for half in range(NY):
                out[lax.rem(yh + half, NY), zs] = total[:, half * width : (half + 1) * width]


def settle(meta, order, parts):
    rows = sum(part[0].shape[0] for part in parts)
    width = parts[0][0].shape[1] // NY
    flat = [array for part in parts for array in part]
    return pl.pallas_call(
        functools.partial(settle_kernel, order),
        in_specs=[pl.BlockSpec(memory_space=pltpu.SMEM)] + [pl.BlockSpec(memory_space=pltpu.VMEM)] * len(flat),
        out_specs=pl.BlockSpec(memory_space=pltpu.VMEM),
        out_shape=jax.ShapeDtypeStruct((NY, NZ, rows // NZ, width), BF16),
        compiler_params=pltpu.CompilerParams(vmem_limit_bytes=VMEM),
    )(meta, *flat)


def shards(queries, stored_keys, stored_values, fresh_keys, fresh_values, cache_lengths, out_weight):
    cache, fresh = stored_keys.shape[0], fresh_keys.shape[0]
    z, yh, core, x, yl = [lax.axis_index(name) for name in AXES]
    meta = jnp.stack([z, yh, core, x, yl]).astype(jnp.int32)

    kv = jnp.concatenate(
        [
            jnp.concatenate([stored_keys, stored_values], 1),
            jnp.concatenate([fresh_keys, fresh_values], 1),
        ],
        0,
    )
    ahead, behind = meet_up(kv), meet_down(kv)
    twin_kv = swap(kv, b=1)

    half = queries.shape[1] // 2
    mine = lax.dynamic_slice_in_dim(queries, core * half, half, 1)
    theirs = swap(lax.dynamic_slice_in_dim(queries, (1 - core) * half, half, 1), b=1)
    near = jnp.concatenate([jnp.where(core == 0, mine, theirs), jnp.where(core == 0, theirs, mine)], 0)
    far = swap(near, a=1)
    q = jnp.concatenate([jnp.where(yh == 0, near, far), jnp.where(yh == 0, far, near)], 0)

    depth = out_weight.shape[0] // 4
    block = lambda value, at, rows: lax.dynamic_slice_in_dim(value, at * rows, rows, 0)
    wide = jnp.concatenate(
        [block(out_weight, core, 2 * depth), swap(block(out_weight, 1 - core, 2 * depth), b=1)], 1
    )
    keep, give = block(wide, yh, depth), block(wide, 1 - yh, depth)
    quarters = [keep, swap(give, a=1), swap(keep, d=1), swap(give, a=1, d=1)]

    def both(ahead, behind, step):
        near = [(ahead, 0, step, 0), (behind, 0, -step, 0)]
        return near + [(swap(array, b=1), at, shift, 1) for array, at, shift, _ in near]

    blocks = [(kv, 0, 0, 0), (twin_kv, 0, 0, 1)] + both(ahead, behind, 1)
    ahead, behind = meet_up(behind), meet_down(ahead)
    blocks += both(ahead, behind, 2)
    ahead, behind = meet_up(behind), meet_down(ahead)
    low = attend(meta, cache_lengths, q, blocks, 0, None, cache, fresh)
    ahead, behind, low = lax.optimization_barrier((ahead, behind, low))
    last_blocks = both(ahead, behind, 3)
    ahead = meet_up(behind)
    low, quarters = lax.optimization_barrier((low, quarters))
    wide = jnp.concatenate(
        [jnp.concatenate(quarters[:2], 1), jnp.concatenate(quarters[2:], 1)], 0
    )
    wide_f, wide_b = shift_x(wide, 1), shift_x(wide, -1)
    high = attend(meta, cache_lengths, q, blocks, 1, None, cache, fresh)
    ahead, high = lax.optimization_barrier((ahead, high))
    last_blocks += [(ahead, 0, 4, 0), (swap(ahead, b=1), 0, 4, 1)]
    pieces = attend(meta, cache_lengths, q, last_blocks, None, (low, high), cache, fresh)

    group, width = pieces.shape[2], pieces.shape[3]
    pieces = lax.all_to_all(
        pieces.reshape(NY * NZ, group, width), ("yh", "x", "yl"), split_axis=0, concat_axis=0, tiled=True
    )
    a = combine(meta, pieces)
    a, wide_f, wide_b = lax.optimization_barrier((a, wide_f, wide_b))
    weights = [wide, wide_b, shift_x(wide_f[:depth], 1), shift_x(wide_b[depth:], -1), wide_f]
    ahead, behind = [a], [a]
    for _ in range(3):
        up, down = meet_up(behind[-1]), meet_down(ahead[-1])
        ahead.append(up)
        behind.append(down)
    ahead.append(meet_up(behind[-1]))

    def share(blocks):
        kept, sent = project(blocks, weights)
        return kept, swap(sent, b=1)

    order = ((0, 1, -1, 2, -2), (3, -3, 4))
    first = share([a, ahead[1], behind[1], ahead[2], behind[2]])
    second = share([ahead[3], behind[3], ahead[4]])
    settled = settle(meta, order, (first, second))
    rows, width = settled.shape[2:]
    home = lax.all_to_all(
        settled.reshape(NY * NZ, rows, width), ("yh", "x", "yl"), split_axis=0, concat_axis=0, tiled=True
    ).reshape(NY, NZ * rows, width)
    return (home[0].astype(F32) + home[1].astype(F32)).astype(BF16)


def solution(mesh):
    split = Mesh(mesh.devices.reshape(NZ, NY, NC, NX, NL), AXES)
    ctx, tp = ("z", "yh", "core"), ("x", "yl")
    spec = P(ctx, tp)
    return jax.shard_map(
        shards,
        mesh=split,
        in_specs=(spec, spec, spec, spec, spec, P(), P(tp, ctx)),
        out_specs=P(tp, ctx),
        check_vma=False,
    )
```

```python
import functools
import math

import jax
import jax.numpy as jnp
from jax import lax
from jax.experimental import pallas as pl
from jax.experimental.pallas import tpu as pltpu
from jax.sharding import Mesh
from jax.sharding import PartitionSpec as P

HEAD = 128
NZ, NY, NC, NX, NL = 8, 2, 2, 4, 2
NEG = -1e30
VMEM = 16 * 1024 * 1024
AXES = ("z", "yh", "core", "x", "yl")
TILE = 256
TAIL = 16
F32 = jnp.float32
BF16 = jnp.bfloat16


def permute(value, move):
    pairs = []
    for z in range(NZ):
        for yh in range(NY):
            for c in range(NC):
                for x in range(NX):
                    for yl in range(NL):
                        z2, yh2, c2, x2, yl2 = move(z, yh, c, x, yl)
                        source = ((z * NY + yh) * NC + c) * NX * NL + x * NL + yl
                        target = (((z2 % NZ) * NY + yh2) * NC + c2) * NX * NL + (x2 % NX) * NL + yl2
                        pairs.append((source, target))
    return lax.ppermute(value, AXES, pairs)


def meet_up(value):
    return permute(value, lambda z, yh, c, x, yl: (z + 1 - 2 * (z % 2), yh, c, x, yl))


def meet_down(value):
    return permute(value, lambda z, yh, c, x, yl: (z - 1 + 2 * (z % 2), yh, c, x, yl))


def shift_x(value, step):
    return permute(value, lambda z, yh, c, x, yl: (z, yh, c, x + step, yl))


def shifted(z, shift):
    return lax.rem(z + shift * (1 - 2 * lax.rem(z, 2)) + NZ, NZ)


def swap(value, a=0, b=0, d=0):
    return permute(value, lambda z, yh, c, x, yl: (z, yh ^ a, c ^ b, x, yl ^ d))


def attend_kernel(sources, heads, which, last, cache, fresh, meta, lens, q_ref, *refs):
    count = len(sources)
    kv_refs, refs = refs[:count], refs[count:]
    rows = q_ref.shape[0]
    group = rows // (NX * NL)
    z, yh, core = meta[0], meta[1], meta[2]
    factor = math.log2(math.e) / math.sqrt(HEAD)

    def head(h, base, before):
        first = before is None
        lanes = pl.ds(pl.multiple_of(h * HEAD, HEAD), HEAD)
        q_lanes = pl.ds(pl.multiple_of((base + h) * HEAD, HEAD), HEAD)

        def score(start):
            q = q_ref[start : start + TILE, q_lanes]
            parts, top = [], None
            for kv, (at, shift, other) in zip(kv_refs, sources):
                span = slice(at * (cache + fresh), (at + 1) * (cache + fresh))
                zs = shifted(z, shift)
                mine = yh * NC + (1 - core if other else core)
                s = lax.dot_general(
                    q, kv[span, :HEAD], (((1,), (1,)), ((), ())), preferred_element_type=F32
                )
                col = lax.broadcasted_iota(jnp.int32, (1, cache), 1)
                stored = s[:, :cache] + jnp.where(col < lens[zs * NY * NC + mine], 0.0, NEG)
                if shift == 0:
                    row = start + lax.broadcasted_iota(jnp.int32, (TILE, fresh), 0)
                    col = mine * fresh + lax.broadcasted_iota(jnp.int32, (TILE, fresh), 1)
                    new = jnp.where(col <= row, s[:, cache:], NEG)
                else:
                    new = s[:, cache:] + jnp.where(zs < z, 0.0, NEG)
                s = jnp.concatenate([stored, new], 1)
                parts.append(s)
                for lane in range(0, cache + fresh, HEAD):
                    piece = s[:, lane : lane + HEAD]
                    top = piece if top is None else jnp.maximum(top, piece)
            return parts, top

        def absorb(start, parts, top):
            here = slice(start, start + TILE)
            m = top.max(axis=1, keepdims=True)
            if first:
                l, acc = None, None
            else:
                acc_in, top_in, sum_in = before
                old = top_in[here, lanes]
                m = jnp.maximum(m, old)
                alpha = jnp.exp2((old - m) * factor)
                m = m[:, 0:1]
                l = sum_in[here, lanes] * alpha
                acc = acc_in[here, lanes] * alpha
            for kv, (at, _, _), s in zip(kv_refs, sources, parts):
                span = slice(at * (cache + fresh), (at + 1) * (cache + fresh))
                p = jnp.exp2((s - m) * factor)
                for lane in range(0, cache + fresh, HEAD):
                    piece = p[:, lane : lane + HEAD]
                    l = piece if l is None else l + piece
                term = jnp.dot(p.astype(BF16), kv[span, HEAD:], preferred_element_type=F32)
                acc = term if acc is None else acc + term
            if not last:
                acc_out, top_out, sum_out = refs[:3]
                acc_out[here, lanes] = acc
                top_out[here, lanes] = jnp.broadcast_to(m, (TILE, HEAD))
                sum_out[here, lanes] = l
                return
            out_ref = refs[-1]
            half = base // heads
            l = l.sum(axis=1, keepdims=True)
            out = (acc / l).astype(BF16)
            lse = m * factor + jnp.log2(l)
            for at in range(0, TILE, group):
                out_ref[half, (start + at) // group, 0:group, lanes] = out[at : at + group, :]
            for at in range(0, TILE, 2 * group):
                line = jnp.broadcast_to(lse[at : at + 2 * group, :], (2 * group, HEAD)).T[0:1, :]
                high = line.astype(BF16).astype(F32)
                middle = (line - high).astype(BF16).astype(F32)
                low = line - high - middle
                kind = lax.broadcasted_iota(jnp.int32, (TAIL, HEAD), 0)
                tail = jnp.where(kind == 0, high, jnp.where(kind == 1, middle, low)).astype(BF16)
                for odd in range(2):
                    out_ref[half, (start + at) // group + odd, group : group + TAIL, lanes] = tail

        starts = list(range(0, rows, TILE))
        now = score(starts[0])
        for at, start in enumerate(starts):
            later = score(starts[at + 1]) if at + 1 < len(starts) else None
            absorb(start, *now)
            now = later
        return 0

    if last:
        for half in range(NY):
            lax.fori_loop(0, heads, lambda h, _: head(h, half * heads, refs[3 * half : 3 * half + 3]), 0)
    else:
        lax.fori_loop(0, heads, lambda h, _: head(h, which * heads, None), 0)


def attend(meta, lens, q, kvs, which, state, cache, fresh):
    rows, width = q.shape
    last = state is not None
    heads = width // HEAD // NY
    span = cache + fresh
    args = [meta, lens, q] + [entry[0] for entry in kvs]
    if last:
        args += [array for half in state for array in half]
        group = rows // (NX * NL)
        out_shape = jax.ShapeDtypeStruct((NY, NX * NL, group + TAIL, heads * HEAD), BF16)
    else:
        out_shape = [jax.ShapeDtypeStruct((rows, heads * HEAD), F32)] * 3
    whole = pl.BlockSpec(memory_space=pltpu.VMEM)
    scalar = pl.BlockSpec(memory_space=pltpu.SMEM)
    out = pl.pallas_call(
        functools.partial(
            attend_kernel, tuple(entry[1:] for entry in kvs), heads, which, last, cache, fresh
        ),
        in_specs=[scalar, scalar] + [whole] * (len(args) - 2),
        out_specs=whole if last else [whole] * 3,
        out_shape=out_shape,
        compiler_params=pltpu.CompilerParams(vmem_limit_bytes=VMEM),
        cost_estimate=pl.CostEstimate(
            flops=4 * rows * heads * HEAD * span * len(kvs) * (2 if last else 1),
            bytes_accessed=4 * rows * width,
            transcendentals=rows * heads * span * len(kvs),
        ),
    )(*args)
    return out if last else tuple(out)


def combine_kernel(group, meta, pieces, out):
    x, yl = meta[3], meta[4]

    def one(t, _):
        spot = lax.rem(t // NL - x + NX, NX) * NL + lax.rem(t + yl, NL)
        for at in range(0, pieces.shape[2], HEAD):
            values, weights = [], []
            for half in range(NY):
                tail = pieces[half * NX * NL + t, group:, at : at + HEAD].astype(F32)
                line = tail[0:1, :] + tail[1:2, :] + tail[2:3, :]
                wide = jnp.broadcast_to(line, (HEAD, HEAD)).T
                weights.append(jnp.where(yl == 0, wide[:group, :], wide[group : 2 * group, :]))
                values.append(pieces[half * NX * NL + t, 0:group, at : at + HEAD].astype(F32))
            top = jnp.maximum(weights[0], weights[1])
            a, b = jnp.exp2(weights[0] - top), jnp.exp2(weights[1] - top)
            joined = (values[0] * a + values[1] * b) / (a + b)
            out[:, pl.ds(pl.multiple_of(spot * pieces.shape[2] + at, HEAD), HEAD)] = joined.astype(BF16)
        return 0

    lax.fori_loop(0, NX * NL, one, 0, unroll=True)


def combine(meta, pieces):
    group, width = pieces.shape[1] - TAIL, pieces.shape[2]
    return pl.pallas_call(
        functools.partial(combine_kernel, group),
        in_specs=[pl.BlockSpec(memory_space=pltpu.SMEM), pl.BlockSpec(memory_space=pltpu.VMEM)],
        out_specs=pl.BlockSpec(memory_space=pltpu.VMEM),
        out_shape=jax.ShapeDtypeStruct((group, NX * NL * width), BF16),
        compiler_params=pltpu.CompilerParams(vmem_limit_bytes=VMEM),
    )(meta, pieces)


def project_kernel(count, *refs):
    blocks, weights, (keep, send) = refs[:count], refs[count:-2], refs[-2:]
    tile = weights[0].shape[1] // (NY * NC)
    for column in range(NY * NC):
        half, core = column // NC, column % NC
        total, at = None, 0
        for weight in weights:
            depth = weight.shape[0]
            a = jnp.concatenate([block[:, at : at + depth] for block in blocks], 0)
            b = weight[:, column * tile : (column + 1) * tile]
            term = jnp.dot(a, b, preferred_element_type=F32)
            total = term if total is None else total + term
            at += depth
        out = keep if core == 0 else send
        out[:, half * tile : (half + 1) * tile] = total.astype(out.dtype)


def project(blocks, weights):
    rows, depth = sum(block.shape[0] for block in blocks), blocks[0].shape[1]
    width = weights[0].shape[1]
    whole = pl.BlockSpec(memory_space=pltpu.VMEM)
    return pl.pallas_call(
        functools.partial(project_kernel, len(blocks)),
        in_specs=[whole] * (len(blocks) + len(weights)),
        out_specs=[whole, whole],
        out_shape=[
            jax.ShapeDtypeStruct((rows, width // NC), F32),
            jax.ShapeDtypeStruct((rows, width // NC), BF16),
        ],
        compiler_params=pltpu.CompilerParams(vmem_limit_bytes=VMEM),
        cost_estimate=pl.CostEstimate(
            flops=2 * rows * depth * width, bytes_accessed=2 * depth * width, transcendentals=0
        ),
    )(*blocks, *weights)


def settle_kernel(order, meta, *refs):
    out = refs[-1]
    width = out.shape[3]
    z, yh = meta[0], meta[1]
    for part, shifts in enumerate(order):
        kept, near = refs[2 * part : 2 * part + 2]
        group = kept.shape[0] // len(shifts)
        for at, shift in enumerate(shifts):
            zs = shifted(z, shift)
            here = pl.ds(at * group, group)
            total = (kept[here, :] + near[here, :].astype(F32)).astype(BF16)
            for half in range(NY):
                out[lax.rem(yh + half, NY), zs] = total[:, half * width : (half + 1) * width]


def settle(meta, order, parts):
    rows = sum(part[0].shape[0] for part in parts)
    width = parts[0][0].shape[1] // NY
    flat = [array for part in parts for array in part]
    return pl.pallas_call(
        functools.partial(settle_kernel, order),
        in_specs=[pl.BlockSpec(memory_space=pltpu.SMEM)] + [pl.BlockSpec(memory_space=pltpu.VMEM)] * len(flat),
        out_specs=pl.BlockSpec(memory_space=pltpu.VMEM),
        out_shape=jax.ShapeDtypeStruct((NY, NZ, rows // NZ, width), BF16),
        compiler_params=pltpu.CompilerParams(vmem_limit_bytes=VMEM),
    )(meta, *flat)


def shards(queries, stored_keys, stored_values, fresh_keys, fresh_values, cache_lengths, out_weight):
    cache, fresh = stored_keys.shape[0], fresh_keys.shape[0]
    z, yh, core, x, yl = [lax.axis_index(name) for name in AXES]
    meta = jnp.stack([z, yh, core, x, yl]).astype(jnp.int32)

    kv = jnp.concatenate(
        [
            jnp.concatenate([stored_keys, stored_values], 1),
            jnp.concatenate([fresh_keys, fresh_values], 1),
        ],
        0,
    )
    ahead, behind = meet_up(kv), meet_down(kv)
    twin_kv = swap(kv, b=1)

    half = queries.shape[1] // 2
    mine = lax.dynamic_slice_in_dim(queries, core * half, half, 1)
    theirs = swap(lax.dynamic_slice_in_dim(queries, (1 - core) * half, half, 1), b=1)
    near = jnp.concatenate([jnp.where(core == 0, mine, theirs), jnp.where(core == 0, theirs, mine)], 0)
    far = swap(near, a=1)
    q = jnp.concatenate([jnp.where(yh == 0, near, far), jnp.where(yh == 0, far, near)], 0)

    depth = out_weight.shape[0] // 4
    block = lambda value, at, rows: lax.dynamic_slice_in_dim(value, at * rows, rows, 0)
    wide = jnp.concatenate(
        [block(out_weight, core, 2 * depth), swap(block(out_weight, 1 - core, 2 * depth), b=1)], 1
    )
    keep, give = block(wide, yh, depth), block(wide, 1 - yh, depth)
    quarters = [keep, swap(give, a=1), swap(keep, d=1), swap(give, a=1, d=1)]

    def both(ahead, behind, step):
        near = [(ahead, 0, step, 0), (behind, 0, -step, 0)]
        return near + [(swap(array, b=1), at, shift, 1) for array, at, shift, _ in near]

    blocks = [(kv, 0, 0, 0), (twin_kv, 0, 0, 1)] + both(ahead, behind, 1)
    ahead, behind = meet_up(behind), meet_down(ahead)
    blocks += both(ahead, behind, 2)
    ahead, behind = meet_up(behind), meet_down(ahead)
    low = attend(meta, cache_lengths, q, blocks, 0, None, cache, fresh)
    ahead, behind, low = lax.optimization_barrier((ahead, behind, low))
    last_blocks = both(ahead, behind, 3)
    ahead = meet_up(behind)
    low, quarters = lax.optimization_barrier((low, quarters))
    wide = jnp.concatenate(
        [jnp.concatenate(quarters[:2], 1), jnp.concatenate(quarters[2:], 1)], 0
    )
    wide_f, wide_b = shift_x(wide, 1), shift_x(wide, -1)
    high = attend(meta, cache_lengths, q, blocks, 1, None, cache, fresh)
    ahead, high = lax.optimization_barrier((ahead, high))
    last_blocks += [(ahead, 0, 4, 0), (swap(ahead, b=1), 0, 4, 1)]
    pieces = attend(meta, cache_lengths, q, last_blocks, None, (low, high), cache, fresh)

    group, width = pieces.shape[2], pieces.shape[3]
    pieces = lax.all_to_all(
        pieces.reshape(NY * NZ, group, width), ("yh", "x", "yl"), split_axis=0, concat_axis=0, tiled=True
    )
    a = combine(meta, pieces)
    a, wide_f, wide_b = lax.optimization_barrier((a, wide_f, wide_b))
    weights = [wide, wide_b, shift_x(wide_f[:depth], 1), shift_x(wide_b[depth:], -1), wide_f]
    ahead, behind = [a], [a]
    for _ in range(3):
        up, down = meet_up(behind[-1]), meet_down(ahead[-1])
        ahead.append(up)
        behind.append(down)
    middle = a.shape[0] // 2
    opposite = [meet_up(behind[-1][:middle]), meet_down(ahead[-1][middle:])]

    def share(blocks):
        kept, sent = project(blocks, weights)
        return kept, swap(sent, b=1)

    order = ((0, 1, -1, 2, -2), (3, -3, 4))
    first = share([a, ahead[1], behind[1], ahead[2], behind[2]])
    second = share([ahead[3], behind[3]] + opposite)
    settled = settle(meta, order, (first, second))
    rows, width = settled.shape[2:]
    home = lax.all_to_all(
        settled.reshape(NY * NZ, rows, width), ("yh", "x", "yl"), split_axis=0, concat_axis=0, tiled=True
    ).reshape(NY, NZ * rows, width)
    return (home[0].astype(F32) + home[1].astype(F32)).astype(BF16)


def solution(mesh):
    split = Mesh(mesh.devices.reshape(NZ, NY, NC, NX, NL), AXES)
    ctx, tp = ("z", "yh", "core"), ("x", "yl")
    spec = P(ctx, tp)
    return jax.shard_map(
        shards,
        mesh=split,
        in_specs=(spec, spec, spec, spec, spec, P(), P(tp, ctx)),
        out_specs=P(tp, ctx),
        check_vma=False,
    )
```
